512 devices in a mesh: dp: 2 (over x_hi), seq: 32 (over z, core), tensor: 8 (over x_lo, y).
Axes of the slice: x: 4 (x_hi: 2, x_lo: 2; x = x_hi * 2 + x_lo), y: 4, z: 16, core: 2. Of those that a mesh axis runs over, the one named last changes fastest.
Arguments:
- queries: bfloat16 [32768, 64, 128], P(('dp', 'seq'), 'tensor'), parts along dimension 0, may hold values from -24 to 24
- keys: bfloat16 [32768, 64, 128], P(('dp', 'seq'), 'tensor'), parts along dimension 0, may hold values from -24 to 24
- values: bfloat16 [32768, 64, 128], P(('dp', 'seq'), 'tensor'), parts along dimension 0, may hold values from -6 to 6
- window_radius: int32 [128], P(('dp', 'tensor')), parts along dimension 0, may hold values from 1 to 3
- global_ids: int32 [4], P('dp'), parts along dimension 0, may hold values from 0 to 255, as said below
- rand_owner: int32 [8, 512, 8, 3], P('tensor', ('dp', 'seq')), parts along dimension 1, may hold values from 0 to 31, all different within a row; in each aligned block of 64 rows (0 to 63, 64 to 127, ..., all dimensions but the last counted through in order) at most 9 rows name the same one
- rand_local: int32 [8, 512, 8, 3], P('tensor', ('dp', 'seq')), parts along dimension 1, may hold values from 0 to 7
Outputs:
- attended: bfloat16 [32768, 64, 128], P(('dp', 'seq'), 'tensor'), parts along dimension 0
The draws below stay inside these ranges and needn't reach their ends.
There are 2 independent parts, one for each index of `dp`. The reference program is written for one: setup_inputs(seed, part) draws one part's arguments, and reference() takes and returns one part's arrays. A program takes and returns all parts, laid end to end along the dimension named above; each array names one. Nothing has to cross between parts.
Inputs may be any that keep to these rules, and one draw needn't show every extreme that they name: `rand_owner`: for the query blocks of one index of seq and the heads of one group, at most 9 random blocks lie in one run; the 3 runs of one query block and head differ. `global_ids`: 2 different block numbers; the last block, 255, is always among them.
All inputs are finite; a program needn't handle non-finite values.
Results may differ from the reference program's by a relative error of at most 0.0046.
Values may be sent and summed in bfloat16 or wider, within the bound.
A program may use at most 128 MiB of HBM per device.

```python
import math
import jax
import jax.numpy as jnp
import numpy as np
from jax import lax

HEADS = 64
HEAD_DIM = 128
BLOCK = 64
WIN = 3
G = 2
R = 3
NB_DEV = 8
HEADS_DEV = 8
GROUPS = 8
SHARDS = 32
NB = 256
SEQ = 16384
CAP = 9


def draw_queries(key, part):
    key = jax.random.fold_in(key, 1)
    shape = (SEQ // 2, 2, HEADS, HEAD_DIM)
    whole = jnp.clip(jax.random.normal(key, shape, jnp.float32), -6.0, 6.0)
    return whole.reshape(SEQ, HEADS, HEAD_DIM).astype(jnp.bfloat16)


def draw_keys(key, part):
    key = jax.random.fold_in(key, 2)
    shape = (SEQ // 2, 2, HEADS, HEAD_DIM)
    whole = jnp.clip(jax.random.normal(key, shape, jnp.float32), -6.0, 6.0)
    return whole.reshape(SEQ, HEADS, HEAD_DIM).astype(jnp.bfloat16)


def draw_global_ids(key, part):
    key = jax.random.fold_in(key, 3)
    last_block = SEQ // BLOCK - 1
    others = jax.random.permutation(key, last_block)[:G - 1].astype(jnp.int32)
    return jnp.concatenate((jnp.full((1,), last_block, jnp.int32), others)).astype(jnp.int32)


def with_ends(entries, own_key, smallest, largest):
    longest = entries.shape.index(max(entries.shape))
    spots = []
    for shift in (0, 1):
        where = [jax.random.randint(jax.random.fold_in(own_key, axis), (), 0, length) for axis, length in enumerate(entries.shape)]
        where[longest] = (where[longest] + shift) % entries.shape[longest]
        spots.append(tuple(where))
    return entries.at[spots[0]].set(smallest).at[spots[1]].set(largest)


def level_of(own_key, dims, split, low, high):
    def one(position, shards_of):
        heights = jax.random.uniform(jax.random.fold_in(jax.random.fold_in(own_key, 6), position), (shards_of,), jnp.float32, low / len(split), high / len(split))
        return jnp.repeat(jnp.exp(heights), dims[position] // shards_of).reshape((-1,) + (1,) * (len(dims) - position - 1))

    level = one(*split[0])
    for cut in split[1:]:
        level = level * one(*cut)
    return level


def shared_out(stream_key, own, number, rows, number_of, top, limit, slope):
    sequence = jax.random.permutation(stream_key, number_of)
    packed, common = shares(number_of, rows * top, limit, slope, True), shares(number_of, rows * top, limit, slope, False)
    places = jnp.arange(number_of)

    def named(lengths, turn):
        used = int((lengths > 0).sum())
        fixed = max(1, used // 4)
        passed = fixed + (places - fixed + turn * (used - fixed)) % max(1, number_of - fixed)
        return jnp.zeros((number_of,), jnp.int32).at[sequence[jnp.where(places < fixed, places, passed)]].set(jnp.asarray(lengths, jnp.int32))

    lengths = jnp.where(number % 4 == 0, named(packed, number // 4), named(common, number - number // 4 - 1))
    mixed = jax.random.permutation(jax.random.fold_in(own, 3), number_of)
    donor, taker = mixed[0:number_of // 2 * 2:2], mixed[1:number_of // 2 * 2:2]
    room = jnp.minimum(lengths[donor] - 1, limit - lengths[taker]) // 2
    room = jnp.where((donor == sequence[0]) | (taker == sequence[0]) | (lengths[taker] == 0), 0, jnp.maximum(room, 0))
    passed = jax.random.randint(jax.random.fold_in(own, 4), (number_of // 2,), 0, 1 << 20) % (room + 1)
    lengths = lengths.at[donor].add(-passed).at[taker].add(passed)
    members = jnp.searchsorted(jnp.cumsum(lengths), jnp.arange(rows * top), side="right").astype(jnp.int32)
    grid = members.reshape(top, rows).T
    grid = grid[jax.random.permutation(jax.random.fold_in(own, 1), rows)]
    turn = jax.random.randint(jax.random.fold_in(own, 2), (rows, 1), 0, top)
    return jnp.take_along_axis(grid, (jnp.arange(top)[None, :] + turn) % top, axis=1)


def shares(count, total, limit, slope, full):
    loads = [(1 << 20) // math.isqrt(standing ** slope) + 1 for standing in range(1, count + 1)]
    largest = limit if full else min(limit, max(-(-total // count), total * loads[0] // sum(loads)))
    least = 1 if total - largest >= count - 1 else 0
    holding, rest = [largest] + [least] * (count - 1), total - largest - least * (count - 1)
    while rest > 0:
        movable = [i for i in range(1, count) if holding[i] < largest] or [i for i in range(1, count) if holding[i] < limit]
        mass, remaining = sum([loads[i] for i in movable]), rest
        for i in movable:
            more = min(limit - holding[i], max(1, remaining * loads[i] // mass), rest)
            holding[i] = holding[i] + more
            rest = rest - more
    return np.array(holding)


def scatter_about(own_key, shape, scale, most, pieces=(), kind=jnp.bfloat16):
    factor_of = level_of(own_key, shape, pieces, -0.22, 0.18) if pieces else 1.0
    values = jax.random.normal(own_key, shape, jnp.float32) * scale * factor_of
    return jnp.minimum(jnp.maximum(values, -most), most).astype(kind)


def setup_inputs(seed: int = 0, part: int = 0) -> dict:
    streams_of = jax.random.split(jax.random.key(seed), 8)
    own_keys = jax.random.split(jax.random.fold_in(streams_of[7], part), 8)
    queries = draw_queries(jax.random.fold_in(jax.random.fold_in(streams_of[7], part), 71), part)
    keys = draw_keys(jax.random.fold_in(jax.random.fold_in(streams_of[7], part), 71), part)
    values = scatter_about(own_keys[2], (SEQ, HEADS, HEAD_DIM), 1.0, 6.0, ((0, 32), (1, 8)))
    window_radius = with_ends(jax.random.randint(own_keys[3], (HEADS,), 1, WIN + 1), jax.random.fold_in(own_keys[3], 1), 1, WIN).astype(jnp.int32)
    global_ids = draw_global_ids(jax.random.fold_in(jax.random.fold_in(streams_of[7], part), 71), part)
    rand_owner_keys = jax.random.split(jax.random.fold_in(own_keys[5], 1), GROUPS * NB * HEADS_DEV // (NB_DEV * HEADS_DEV))
    rand_owner_turns = jax.random.permutation(jax.random.fold_in(own_keys[5], 3), GROUPS * NB * HEADS_DEV // (NB_DEV * HEADS_DEV))
    rand_owner = jax.vmap(lambda own, number: shared_out(jax.random.fold_in(own_keys[5], 2), own, number, NB_DEV * HEADS_DEV, SHARDS, R, CAP, 2))(rand_owner_keys, rand_owner_turns).reshape((GROUPS, NB, HEADS_DEV, R))
    rand_local = with_ends(jax.random.randint(own_keys[6], (GROUPS, NB, HEADS_DEV, R), 0, NB_DEV), jax.random.fold_in(own_keys[6], 1), 0, NB_DEV - 1).astype(jnp.int32)
    return dict(queries=queries, keys=keys, values=values, window_radius=window_radius, global_ids=global_ids, rand_owner=rand_owner, rand_local=rand_local)


def reference(queries, keys, values, window_radius, global_ids, rand_owner, rand_local):
    total_blocks = SEQ // BLOCK
    score_scale = 1.0 / math.sqrt(HEAD_DIM)
    random_table = (rand_owner * NB_DEV + rand_local).transpose(1, 0, 2, 3).reshape(total_blocks, HEADS, R)
    random_table = random_table.astype(jnp.int32)

    def head_attention(items):
        query_head, key_head, value_head, radius, random_blocks = items
        query_blocks = query_head.reshape(total_blocks, BLOCK, HEAD_DIM)
        key_blocks = key_head.reshape(total_blocks, BLOCK, HEAD_DIM)
        value_blocks = value_head.reshape(total_blocks, BLOCK, HEAD_DIM)
        offsets = jnp.arange(-WIN, WIN + 1, dtype=jnp.int32)
        window = jnp.arange(total_blocks, dtype=jnp.int32)[:, None] + offsets[None, :]
        inside = (window >= 0) & (window < total_blocks) & (jnp.abs(offsets) <= radius)[None, :]
        window = jnp.clip(window, 0, total_blocks - 1)
        chosen = jnp.concatenate((window, jnp.broadcast_to(global_ids[None, :], (total_blocks, G)).astype(jnp.int32), random_blocks.astype(jnp.int32)), axis=1)
        usable = jnp.concatenate((inside, jnp.ones((total_blocks, G + R), jnp.bool_)), axis=1)
        usable_mask = usable[:, None, :, None]
        gathered_keys = key_blocks[chosen].astype(jnp.float32)
        gathered_values = value_blocks[chosen].astype(jnp.float32)
        scores = jnp.einsum('btd,bkjd->btkj', query_blocks.astype(jnp.float32), gathered_keys) * score_scale
        row_peak = lax.optimization_barrier(jnp.max(jnp.where(usable_mask, scores, -jnp.inf), axis=(2, 3), keepdims=True))
        weights = jnp.where(usable_mask, jnp.exp(scores - row_peak), 0.0)
        row_total = lax.optimization_barrier(jnp.sum(weights, axis=(2, 3)))
        rounded = weights.astype(jnp.bfloat16).astype(jnp.float32)
        weighted = jnp.einsum('btkj,bkjd->btd', rounded, gathered_values)
        sparse_out = weighted / row_total[..., None]
        global_queries = query_blocks[global_ids].astype(jnp.float32)
        global_scores = jnp.einsum('gtd,sd->gts', global_queries, key_head.astype(jnp.float32)) * score_scale
        global_peak = lax.optimization_barrier(jnp.max(global_scores, axis=-1, keepdims=True))
        global_weights = jnp.exp(global_scores - global_peak)
        global_total = lax.optimization_barrier(jnp.sum(global_weights, axis=-1))
        global_rounded = global_weights.astype(jnp.bfloat16).astype(jnp.float32)
        global_weighted = jnp.einsum('gts,sd->gtd', global_rounded, value_head.astype(jnp.float32))
        global_out = global_weighted / global_total[..., None]
        merged = sparse_out.at[global_ids].set(global_out)
        return merged.reshape(SEQ, HEAD_DIM).astype(jnp.bfloat16)
    per_head = lax.map(head_attention, (queries.transpose(1, 0, 2), keys.transpose(1, 0, 2), values.transpose(1, 0, 2), window_radius, random_table.transpose(1, 0, 2)))
    return per_head.transpose(1, 0, 2)
```

```python
import math

import jax
import jax.numpy as jnp
from jax import lax
from jax.experimental import pallas as pl
from jax.experimental.pallas import tpu as pltpu
from jax.sharding import PartitionSpec as P

BLOCK = 64
WIN = 3
G = 2
R = 3
NB_DEV = 8
HEADS = 8
WIDTH = 128
SPAN = (NB_DEV + 2 * WIN) * BLOCK
WKEYS = (2 * WIN + 1) * BLOCK
FETCH = G + NB_DEV * R


def attend_kernel(spot, info, query, key_run, value_run, pool, out, fetched, sems):
    head = pl.program_id(0)

    def copies(which, slot):
        for i in range(FETCH):
            yield pltpu.make_async_copy(
                pool.at[spot[which * FETCH + i]], fetched.at[slot, i], sems.at[slot, i]
            )

    @pl.when(head == 0)
    def _():
        for copy in copies(0, 0):
            copy.start()

    @pl.when(head + 1 < HEADS)
    def _():
        for copy in copies(head + 1, (head + 1) % 2):
            copy.start()

    slot = head % 2
    for copy in copies(head, slot):
        copy.wait()
    radius = info[head]
    first = info[HEADS]
    total = info[HEADS + 1]
    column = lax.broadcasted_iota(jnp.int32, (1, WKEYS), 1) // BLOCK - WIN

    def one_block(b, carry):
        rows = pl.ds(pl.multiple_of(b * BLOCK, BLOCK), BLOCK)
        span = pl.ds(pl.multiple_of(b * BLOCK, BLOCK), WKEYS)
        q = query[0, rows]
        others = [0, 1] + [G + b * R + r for r in range(R)]
        far_keys = jnp.concatenate([fetched[slot, i, 0] for i in others], axis=0)
        far_values = jnp.concatenate([fetched[slot, i, 1] for i in others], axis=0)
        target = first + b + column
        usable = (jnp.abs(column) <= radius) & (target >= 0) & (target < total)
        contract = (((1,), (1,)), ((), ()))
        scale = 1.0 / math.sqrt(WIDTH)
        near = lax.dot_general(
            q, key_run[0, span], contract, preferred_element_type=jnp.float32
        )
        near = jnp.where(usable, near * scale, -jnp.inf)
        far = lax.dot_general(q, far_keys, contract, preferred_element_type=jnp.float32) * scale
        peak = jnp.maximum(
            jnp.max(near, axis=1, keepdims=True), jnp.max(far, axis=1, keepdims=True)
        )
        near = jnp.exp(near - peak)
        far = jnp.exp(far - peak)
        row_total = jnp.sum(near, axis=1, keepdims=True) + jnp.sum(far, axis=1, keepdims=True)
        weighted = jnp.dot(
            near.astype(jnp.bfloat16), value_run[0, span], preferred_element_type=jnp.float32
        ) + jnp.dot(far.astype(jnp.bfloat16), far_values, preferred_element_type=jnp.float32)
        out[0, rows] = (weighted / row_total).astype(jnp.bfloat16)
        return carry

    lax.fori_loop(0, NB_DEV, one_block, 0, unroll=2)


def attend(spot, info, query, key_run, value_run, pool):
    per_head = lambda rows: pl.BlockSpec((1, rows, WIDTH), lambda h, *_: (h, 0, 0))
    return pl.pallas_call(
        attend_kernel,
        grid_spec=pltpu.PrefetchScalarGridSpec(
            num_scalar_prefetch=2,
            grid=(HEADS,),
            in_specs=[
                per_head(NB_DEV * BLOCK),
                per_head(SPAN),
                per_head(SPAN),
                pl.BlockSpec(memory_space=pl.ANY),
            ],
            out_specs=per_head(NB_DEV * BLOCK),
            scratch_shapes=[
                pltpu.VMEM((2, FETCH, 2, BLOCK, WIDTH), jnp.bfloat16),
                pltpu.SemaphoreType.DMA((2, FETCH)),
            ],
        ),
        out_shape=jax.ShapeDtypeStruct((HEADS, NB_DEV * BLOCK, WIDTH), jnp.bfloat16),
        compiler_params=pltpu.CompilerParams(vmem_limit_bytes=32 * 1024 * 1024),
        name="attend",
    )(spot, info, query, key_run, value_run, pool)


def with_halo(block, width):
    count = lax.axis_size("seq")
    forward = [(i, i + 1) for i in range(count - 1)]
    backward = [(target, source) for source, target in forward]
    low = lax.ppermute(block[:, :, -width:], "seq", forward)
    high = lax.ppermute(block[:, :, :width], "seq", backward)
    return jnp.concatenate([low, block, high], axis=2)


def local(queries, keys, values, window_radius, global_ids, rand_owner, rand_local):
    shards = lax.axis_size("seq")
    position = lax.axis_index("seq")
    score_scale = 1.0 / math.sqrt(WIDTH)
    block_ids = position * NB_DEV + jnp.arange(NB_DEV, dtype=jnp.int32)

    by_head = jnp.stack((keys, values)).transpose(0, 2, 1, 3)
    pairs = by_head.reshape(2, HEADS, NB_DEV, BLOCK, WIDTH).transpose(1, 2, 0, 3, 4)
    pairs = pairs.reshape(HEADS * NB_DEV, 2, BLOCK, WIDTH)
    runs = with_halo(by_head, WIN * BLOCK)
    query_heads = queries.transpose(1, 0, 2)
    pool = lax.all_gather(pairs, "seq", axis=0, tiled=True)

    blocks_query = queries.reshape(NB_DEV, BLOCK * HEADS * WIDTH)
    selector = (global_ids[:, None] == block_ids[None, :]).astype(jnp.bfloat16)
    picked = jnp.einsum("gb,bf->gf", selector, blocks_query, preferred_element_type=jnp.float32)
    global_query = lax.psum(picked.astype(jnp.bfloat16), "seq").reshape(G, BLOCK, HEADS, WIDTH)
    global_scores = (
        jnp.einsum("gthd,hsd->hgts", global_query, by_head[0], preferred_element_type=jnp.float32)
        * score_scale
    )
    global_peak = lax.pmax(jnp.max(global_scores, axis=-1), "seq")
    global_weights = jnp.exp(global_scores - global_peak[..., None])
    local_total = jnp.sum(global_weights, axis=-1)
    local_weighted = jnp.einsum(
        "hgts,hsd->hgtd",
        global_weights.astype(jnp.bfloat16),
        by_head[1],
        preferred_element_type=jnp.float32,
    )
    global_total, global_weighted = lax.psum((local_total, local_weighted), "seq")
    global_out = (global_weighted / global_total[..., None]).astype(jnp.bfloat16)

    heads = jnp.arange(HEADS, dtype=jnp.int32)
    random_spot = rand_owner[0] * (HEADS * NB_DEV) + heads[None, :, None] * NB_DEV + rand_local[0]
    random_spot = random_spot.transpose(1, 0, 2).reshape(HEADS, NB_DEV * R)
    global_spot = (
        (global_ids // NB_DEV)[None, :] * (HEADS * NB_DEV)
        + heads[:, None] * NB_DEV
        + (global_ids % NB_DEV)[None, :]
    )
    spot = jnp.concatenate((global_spot, random_spot), axis=1).reshape(-1)
    info = jnp.concatenate(
        (window_radius, jnp.stack((position * NB_DEV, jnp.int32(shards * NB_DEV))))
    ).astype(jnp.int32)
    sparse = attend(spot, info, query_heads, runs[0], runs[1], pool)

    result = sparse.reshape(HEADS, NB_DEV, BLOCK, WIDTH).transpose(1, 2, 0, 3)
    for slot in range(G):
        owned = global_ids[slot] == block_ids
        result = jnp.where(
            owned[:, None, None, None], global_out[:, slot].transpose(1, 0, 2)[None], result
        )
    return result.reshape(NB_DEV * BLOCK, HEADS, WIDTH)


def solution(mesh):
    placed = (
        P(("dp", "seq"), "tensor", None),
        P(("dp", "seq"), "tensor", None),
        P(("dp", "seq"), "tensor", None),
        P(("dp", "tensor")),
        P("dp"),
        P("tensor", ("dp", "seq"), None, None),
        P("tensor", ("dp", "seq"), None, None),
    )
    return jax.shard_map(
        local,
        mesh=mesh,
        in_specs=placed,
        out_specs=P(("dp", "seq"), "tensor", None),
        check_vma=False,
    )
```

```python
import math

import jax
import jax.numpy as jnp
from jax import lax
from jax.experimental import pallas as pl
from jax.experimental.pallas import tpu as pltpu
from jax.sharding import PartitionSpec as P

BLOCK = 64
WIN = 3
G = 2
R = 3
NB_DEV = 8
HEADS = 8
WIDTH = 128
SPAN = (NB_DEV + 2 * WIN) * BLOCK
WKEYS = (2 * WIN + 1) * BLOCK
PICKS = NB_DEV * R
FETCH = G + PICKS

RUNS = 32
CHIPS = 16
OWN = HEADS * NB_DEV
QUNITS = 8
UNITS = 2 * QUNITS + 2 * OWN
SLOTS = 8
PHASES = 37
PIECES = 4
PIECE = SLOTS // PIECES
STAGES = 4
ENTRIES = 2 * PHASES * 2 * SLOTS
UNIT = (2, BLOCK, WIDTH)
MESH = pl.DeviceIdType.MESH


def place(seq):
    return (lax.axis_index("dp"), seq, lax.axis_index("tensor"))


def greet(devices):
    barrier = pltpu.get_barrier_semaphore()
    for device in devices:
        pl.semaphore_signal(barrier, inc=1, device_id=device, device_id_type=MESH)
    pl.semaphore_wait(barrier, len(devices))


def exchange_kernel(wanted, pairs, units, table, pool, send, land, own_sem, pair_send, pair_land):
    me = lax.axis_index("seq")
    side = lax.rem(me, 2)
    sibling = me + 1 - 2 * side
    peers = [lax.rem(me + k, RUNS) for k in range(1, RUNS)]
    greet([place(peer) for peer in peers])
    parts = (
        (units, lambda who: pl.ds(who * QUNITS, QUNITS)),
        (pairs, lambda who: pl.ds(2 * QUNITS + who * OWN, OWN)),
    )

    def across(i, who):
        source, rows = parts[i]
        return pltpu.make_async_remote_copy(
            src_ref=source,
            dst_ref=pool.at[rows(who)],
            send_sem=pair_send.at[i],
            recv_sem=pair_land.at[i],
            device_id=place(sibling),
            device_id_type=MESH,
        )

    def tell(k, slot):
        return pltpu.make_async_remote_copy(
            src_ref=wanted,
            dst_ref=table.at[slot],
            send_sem=send.at[k],
            recv_sem=land.at[k],
            device_id=place(lax.rem(me + k, RUNS)),
            device_id_type=MESH,
        )

    for k in range(1, RUNS):
        tell(k, me).start()
    kept = [pltpu.make_async_copy(wanted, table.at[me], own_sem.at[2])]
    for i in range(2):
        across(i, side).start()
        kept.append(pltpu.make_async_copy(parts[i][0], pool.at[parts[i][1](side)], own_sem.at[i]))
    for copy in kept:
        copy.start()
    for k in range(1, RUNS):
        tell(k, me).wait_send()
        tell(k, lax.rem(me + RUNS - k, RUNS)).wait_recv()
    for i in range(2):
        across(i, side).wait_send()
        across(i, 1 - side).wait_recv()
    for copy in kept:
        copy.wait()


def exchange(wanted, pairs, units):
    dma = pltpu.SemaphoreType.DMA
    return pl.pallas_call(
        exchange_kernel,
        in_specs=[
            pl.BlockSpec(memory_space=pltpu.VMEM),
            pl.BlockSpec(memory_space=pl.ANY),
            pl.BlockSpec(memory_space=pl.ANY),
        ],
        out_specs=(
            pl.BlockSpec(memory_space=pltpu.VMEM),
            pl.BlockSpec(memory_space=pl.ANY),
        ),
        out_shape=(
            jax.ShapeDtypeStruct((RUNS, HEADS, WIDTH), jnp.int32),
            jax.ShapeDtypeStruct((UNITS,) + UNIT, jnp.bfloat16),
        ),
        scratch_shapes=[
            dma((RUNS,)),
            dma((RUNS,)),
            dma((3,)),
            dma((2,)),
            dma((2,)),
        ],
        compiler_params=pltpu.CompilerParams(collective_id=0, has_side_effects=True),
        name="exchange",
    )(wanted, pairs, units)


def schedule_kernel(counts, taken, landed, rest):
    lane = lax.broadcasted_iota(jnp.int32, (2 * SLOTS, 128), 1)
    row = lax.broadcasted_iota(jnp.int32, (2 * SLOTS, 128), 0)
    wrap = lane % CHIPS == 0
    reach = [jnp.broadcast_to(counts[p : p + 1, :], (2 * SLOTS, 128)) for p in range(8)]

    def shift(x):
        return jnp.where(wrap, pltpu.roll(x, 128 - CHIPS + 1, 1), pltpu.roll(x, 1, 1))

    def phase(t, state):
        left, code, queue = state
        free = left == 0
        running = free.astype(jnp.int32)
        for step in (1, 2, 4, 8):
            running = running + jnp.where(row >= step, pltpu.roll(running, step, 0), 0)
        number = queue + running - free.astype(jnp.int32)
        fresh = free & (number < reach[0])
        extent = sum((number < reach[p]).astype(jnp.int32) for p in range(8))
        left = jnp.where(fresh, extent, left)
        code = jnp.where(fresh, lane * 256 + number, code)
        taken[t] = jnp.where(fresh, number, -1)
        used = jnp.sum(free.astype(jnp.int32), axis=0, keepdims=True)
        queue = jnp.minimum(queue + used, reach[0])
        left = shift(left)
        code = shift(code)
        landed[t] = jnp.where(left > 0, code, -1)
        return jnp.maximum(left - 1, 0), code, queue

    zero = jnp.zeros((2 * SLOTS, 128), jnp.int32)
    left, code, queue = lax.fori_loop(0, PHASES, phase, (zero, zero, zero))
    rest[...] = left + reach[0] - queue


def schedule(counts):
    return pl.pallas_call(
        schedule_kernel,
        out_shape=(
            jax.ShapeDtypeStruct((PHASES, 2 * SLOTS, 128), jnp.int32),
            jax.ShapeDtypeStruct((PHASES, 2 * SLOTS, 128), jnp.int32),
            jax.ShapeDtypeStruct((2 * SLOTS, 128), jnp.int32),
        ),
        name="schedule",
    )(counts)


def plan(table, global_ids):
    position = lax.axis_index("seq")
    chip, side = position // 2, position % 2
    codes = jnp.arange(RUNS * NB_DEV, dtype=jnp.int32)
    hit = jnp.any(table[:, :, :PICKS, None] == codes, axis=2)
    everywhere = jnp.any(codes[None, :] == global_ids[:, None], axis=0)
    hit = hit | everywhere
    delta = (jnp.arange(RUNS, dtype=jnp.int32)[:, None] // 2 - codes[None, :] // 16) & (CHIPS - 1)
    delta = delta[:, None, :]
    right = jnp.max(jnp.where(hit & (delta < 8), delta, 0), axis=0)
    left = jnp.max(jnp.where(hit & (delta > 8), CHIPS - delta, 0), axis=0)
    far = jnp.any(hit & (delta == 8), axis=0)
    even = (jnp.arange(HEADS, dtype=jnp.int32)[:, None] + codes[None, :]) % 2 == 0
    by_right = (right > left) | ((right == left) & even)
    extent = jnp.stack((jnp.where(far & by_right, 8, right), jnp.where(far & ~by_right, 8, left)))
    extent = extent.reshape(2, HEADS, CHIPS, 2, NB_DEV).transpose(0, 2, 3, 1, 4)
    extent = extent.reshape(2, CHIPS, 2 * OWN)
    holder = jnp.arange(RUNS, dtype=jnp.int32).reshape(CHIPS, 2, 1)
    unit_holder = jnp.repeat(global_ids // NB_DEV, QUNITS // G)
    query_extent = jnp.where(holder == unit_holder, 8, 0).reshape(CHIPS, 2 * QUNITS)
    extent = jnp.concatenate((jnp.stack((query_extent,) * 2), extent), axis=2)
    index = jnp.arange(UNITS, dtype=jnp.int32)
    ahead = (extent[:, :, None, :] > extent[:, :, :, None]) | (
        (extent[:, :, None, :] == extent[:, :, :, None]) & (index[None, :] < index[:, None])
    )
    rank = jnp.sum(ahead.astype(jnp.int32), axis=3)
    reach = jnp.arange(1, 9, dtype=jnp.int32)[:, None, None, None]
    counts = jnp.sum((extent[None] >= reach).astype(jnp.int32), axis=3)
    counts = jnp.concatenate((counts[:, 0], counts[:, 1, ::-1]), axis=1)
    counts = jnp.pad(counts, ((0, 0), (0, 128 - 2 * CHIPS)))
    taken, landed, rest = schedule(counts)

    def mine(x):
        pick = lambda lane: lax.dynamic_index_in_dim(x, lane, axis=2, keepdims=False)
        both = jnp.stack((pick(chip), pick(2 * CHIPS - 1 - chip)))
        return both.reshape(2, PHASES, SLOTS, 2).transpose(0, 1, 3, 2)

    own_rank = lax.dynamic_index_in_dim(rank, chip, axis=1, keepdims=False)
    own_taken = lax.dynamic_index_in_dim(mine(taken), side, axis=2, keepdims=False)
    same = own_rank[:, None, None, :] == own_taken[..., None]
    source = jnp.sum(jnp.where(same, index + 1, 0), axis=3) - 1
    arrived = mine(landed).reshape(2, 1, 1, ENTRIES // 2)
    chips = jnp.arange(CHIPS, dtype=jnp.int32)
    origin = jnp.stack((chips, 2 * CHIPS - 1 - chips))
    token = origin[:, :, None] * 256 + rank
    entry = jnp.arange(ENTRIES, dtype=jnp.int32).reshape(2, 1, 1, ENTRIES // 2)
    where = jnp.max(jnp.where(token[..., None] == arrived, entry, 0), axis=(0, 3))
    where = jnp.where((chips == chip)[:, None], ENTRIES + index[None, :], where)
    return source.reshape(-1), where.reshape(-1), rest


def packet_kernel(
    source, pool, rest, log, flag, recv, stage, votes,
    send_sem, land_sem, keep_sem, across_sem, across_land, tail_sem, vote_send, vote_land,
):
    me = lax.axis_index("seq")
    chip, side = me // 2, lax.rem(me, 2)
    sibling = me + 1 - 2 * side
    ahead = lax.rem(chip + 1, CHIPS) * 2 + side
    behind = lax.rem(chip + CHIPS - 1, CHIPS) * 2 + side
    dp, tensor = lax.axis_index("dp"), lax.axis_index("tensor")
    ring = dp * 8 + tensor

    def other(k):
        there = lax.rem(ring + k, 16)
        return (there // 8, me, lax.rem(there, 8))

    greet([place(ahead), place(behind), place(sibling)] + [other(k) for k in range(1, 16)])

    def vote(k, slot):
        return pltpu.make_async_remote_copy(
            src_ref=rest,
            dst_ref=votes.at[slot],
            send_sem=vote_send.at[k],
            recv_sem=vote_land.at[k],
            device_id=other(k),
            device_id_type=MESH,
        )

    for k in range(1, 16):
        vote(k, ring).start()
    tail = pltpu.make_async_copy(pool, log.at[pl.ds(ENTRIES, UNITS)], tail_sem.at[0])
    tail.start()
    own_vote = pltpu.make_async_copy(rest, votes.at[ring], tail_sem.at[1])
    own_vote.start()

    def hop(t, way, piece):
        rows = pl.ds(piece * PIECE, PIECE)
        return pltpu.make_async_remote_copy(
            src_ref=stage.at[way, lax.rem(t, STAGES), rows],
            dst_ref=recv.at[way, t, rows],
            send_sem=send_sem.at[way, lax.rem(t, STAGES), piece],
            recv_sem=land_sem.at[way, t, piece],
            device_id=place(ahead if way == 0 else behind),
            device_id_type=MESH,
        )

    def entry(t, way, piece, who):
        return pl.ds(((way * PHASES + t) * 2 + who) * SLOTS + piece * PIECE, PIECE)

    def keep(t, way, piece):
        return pltpu.make_async_copy(
            recv.at[way, t, pl.ds(piece * PIECE, PIECE)],
            log.at[entry(t, way, piece, side)],
            keep_sem.at[way, lax.rem(t, 2), piece],
        )

    def across(t, way, piece, who):
        return pltpu.make_async_remote_copy(
            src_ref=recv.at[way, t, pl.ds(piece * PIECE, PIECE)],
            dst_ref=log.at[entry(t, way, piece, who)],
            send_sem=across_sem.at[way, lax.rem(t, 2), piece],
            recv_sem=across_land.at[way, t, piece],
            device_id=place(sibling),
            device_id_type=MESH,
        )

    def compose(t, way, piece, first):
        for i in range(PIECE):
            slot = piece * PIECE + i
            wanted = source[(way * PHASES + t) * SLOTS + slot]
            unit = pool[jnp.maximum(wanted, 0)]
            if not first:
                unit = jnp.where(wanted >= 0, unit, recv[way, t - 1, slot])
            stage[way, lax.rem(t, STAGES), slot] = unit

    for piece in range(PIECES):
        for way in range(2):
            compose(0, way, piece, True)
            hop(0, way, piece).start()

    def arrive(t, way, piece):
        hop(t, way, piece).wait_recv()

        def settle():
            keep(t - 2, way, piece).wait()
            across(t - 2, way, piece, side).wait_send()

        pl.when(t >= 2)(settle)

    def pass_on(t, way, piece):
        keep(t, way, piece).start()
        across(t, way, piece, side).start()

    def phase(t, carry):
        def step(piece, inner):
            for way in range(2):
                arrive(t - 1, way, piece)
                pl.when(t >= STAGES)(lambda: hop(t - STAGES, way, piece).wait_send())
                compose(t, way, piece, False)
                hop(t, way, piece).start()
                pass_on(t - 1, way, piece)
            return inner

        return lax.fori_loop(0, PIECES, step, carry)

    lax.fori_loop(1, PHASES, phase, 0)

    def last(piece, carry):
        for way in range(2):
            arrive(PHASES - 1, way, piece)
            pass_on(PHASES - 1, way, piece)
            for t in range(PHASES - STAGES, PHASES):
                hop(t, way, piece).wait_send()
            for t in (PHASES - 2, PHASES - 1):
                keep(t, way, piece).wait()
                across(t, way, piece, side).wait_send()
        return carry

    lax.fori_loop(0, PIECES, last, 0)

    def drain(t, carry):
        def step(piece, inner):
            for way in range(2):
                across(t, way, piece, 1 - side).wait_recv()
            return inner

        return lax.fori_loop(0, PIECES, step, carry)

    lax.fori_loop(0, PHASES, drain, 0)
    for k in range(1, 16):
        vote(k, ring).wait_send()
        vote(k, lax.rem(ring + 16 - k, 16)).wait_recv()
    tail.wait()
    own_vote.wait()
    flag[...] = jnp.max(votes[...], axis=0)


def packets(source, pool, rest):
    dma = pltpu.SemaphoreType.DMA
    vmem = pl.BlockSpec(memory_space=pltpu.VMEM)
    return pl.pallas_call(
        packet_kernel,
        in_specs=[pl.BlockSpec(memory_space=pltpu.SMEM), vmem, vmem],
        out_specs=(pl.BlockSpec(memory_space=pl.ANY), vmem),
        out_shape=(
            jax.ShapeDtypeStruct((ENTRIES + UNITS,) + UNIT, jnp.bfloat16),
            jax.ShapeDtypeStruct((2 * SLOTS, 128), jnp.int32),
        ),
        scratch_shapes=[
            pltpu.VMEM((2, PHASES, SLOTS) + UNIT, jnp.bfloat16),
            pltpu.VMEM((2, STAGES, SLOTS) + UNIT, jnp.bfloat16),
            pltpu.VMEM((16, 2 * SLOTS, 128), jnp.int32),
            dma((2, STAGES, PIECES)),
            dma((2, PHASES, PIECES)),
            dma((2, 2, PIECES)),
            dma((2, 2, PIECES)),
            dma((2, PHASES, PIECES)),
            dma((2,)),
            dma((16,)),
            dma((16,)),
        ],
        compiler_params=pltpu.CompilerParams(
            collective_id=1, has_side_effects=True, vmem_limit_bytes=48 * 1024 * 1024
        ),
        name="packets",
    )(source, pool, rest)


def attend_kernel(
    fast, where, wanted, info, query, key_run, value_run, pool, query_pool, out, part, stats,
    fetched, asked, sems, asked_sems,
):
    head = pl.program_id(0)

    def spot(code, h):
        low = code & (NB_DEV - 1)
        if fast:
            inner = 2 * QUNITS + ((code >> 3) & 1) * OWN + h * NB_DEV + low
            return where[(code >> 4) * UNITS + inner]
        return (code >> 3) * OWN + h * NB_DEV + low

    def query_spot(g, h):
        unit = g * (QUNITS // G) + h // 2
        if fast:
            code = info[HEADS + 2 + g]
            return where[(code >> 4) * UNITS + ((code >> 3) & 1) * QUNITS + unit]
        return unit

    def copies(h, slot):
        for i in range(FETCH):
            code = info[HEADS + 2 + i] if i < G else wanted[h * PICKS + i - G]
            yield pltpu.make_async_copy(
                pool.at[spot(code, h)], fetched.at[slot, i], sems.at[slot, i]
            )
        for g in range(G):
            yield pltpu.make_async_copy(
                query_pool.at[query_spot(g, h), h % 2], asked.at[slot, g], asked_sems.at[slot, g]
            )

    @pl.when(head == 0)
    def _():
        for copy in copies(head, 0):
            copy.start()

    @pl.when(head + 1 < HEADS)
    def _():
        for copy in copies(head + 1, (head + 1) % 2):
            copy.start()

    slot = head % 2
    for copy in copies(head, slot):
        copy.wait()
    radius = info[head]
    first = info[HEADS]
    total = info[HEADS + 1]
    column = lax.broadcasted_iota(jnp.int32, (1, WKEYS), 1) // BLOCK - WIN
    contract = (((1,), (1,)), ((), ()))
    scale = 1.0 / math.sqrt(WIDTH)

    own = pl.ds(WIN * BLOCK, NB_DEV * BLOCK)
    scores = scale * lax.dot_general(
        key_run[0, own],
        asked[slot].reshape(G * BLOCK, WIDTH),
        contract,
        preferred_element_type=jnp.float32,
    )
    peak = jnp.max(scores, axis=0, keepdims=True)
    weights = jnp.exp(scores - peak)
    sums = jnp.sum(weights, axis=0, keepdims=True)
    weighted = lax.dot_general(
        value_run[0, own],
        weights.astype(jnp.bfloat16),
        (((0,), (0,)), ((), ())),
        preferred_element_type=jnp.float32,
    )
    part[0] = (weighted / sums).astype(jnp.bfloat16)
    stats[0] = jnp.concatenate((peak, sums, jnp.zeros((6, WIDTH), jnp.float32)), axis=0)

    def one_block(b, carry):
        rows = pl.ds(pl.multiple_of(b * BLOCK, BLOCK), BLOCK)
        span = pl.ds(pl.multiple_of(b * BLOCK, BLOCK), WKEYS)
        q = query[0, rows]
        others = [0, 1] + [G + b * R + r for r in range(R)]
        far_keys = jnp.concatenate([fetched[slot, i, 0] for i in others], axis=0)
        far_values = jnp.concatenate([fetched[slot, i, 1] for i in others], axis=0)
        target = first + b + column
        usable = (jnp.abs(column) <= radius) & (target >= 0) & (target < total)
        near = lax.dot_general(
            q, key_run[0, span], contract, preferred_element_type=jnp.float32
        )
        near = jnp.where(usable, near * scale, -jnp.inf)
        far = lax.dot_general(q, far_keys, contract, preferred_element_type=jnp.float32) * scale
        peak = jnp.maximum(
            jnp.max(near, axis=1, keepdims=True), jnp.max(far, axis=1, keepdims=True)
        )
        near = jnp.exp(near - peak)
        far = jnp.exp(far - peak)
        row_total = jnp.sum(near, axis=1, keepdims=True) + jnp.sum(far, axis=1, keepdims=True)
        weighted = jnp.dot(
            near.astype(jnp.bfloat16), value_run[0, span], preferred_element_type=jnp.float32
        ) + jnp.dot(far.astype(jnp.bfloat16), far_values, preferred_element_type=jnp.float32)
        out[0, rows] = (weighted / row_total).astype(jnp.bfloat16)
        return carry

    lax.fori_loop(0, NB_DEV, one_block, 0, unroll=2)


def attend(fast, where, wanted, info, query, key_run, value_run, pool, query_pool):
    per_head = lambda rows: pl.BlockSpec((1, rows, WIDTH), lambda h, *_: (h, 0, 0))
    return pl.pallas_call(
        lambda *refs: attend_kernel(fast, *refs),
        grid_spec=pltpu.PrefetchScalarGridSpec(
            num_scalar_prefetch=3,
            grid=(HEADS,),
            in_specs=[
                per_head(NB_DEV * BLOCK),
                per_head(SPAN),
                per_head(SPAN),
                pl.BlockSpec(memory_space=pl.ANY),
                pl.BlockSpec(memory_space=pl.ANY),
            ],
            out_specs=(per_head(NB_DEV * BLOCK), per_head(WIDTH), per_head(8)),
            scratch_shapes=[
                pltpu.VMEM((2, FETCH) + UNIT, jnp.bfloat16),
                pltpu.VMEM((2, G, BLOCK, WIDTH), jnp.bfloat16),
                pltpu.SemaphoreType.DMA((2, FETCH)),
                pltpu.SemaphoreType.DMA((2, G)),
            ],
        ),
        out_shape=(
            jax.ShapeDtypeStruct((HEADS, NB_DEV * BLOCK, WIDTH), jnp.bfloat16),
            jax.ShapeDtypeStruct((HEADS, WIDTH, G * BLOCK), jnp.bfloat16),
            jax.ShapeDtypeStruct((HEADS, 8, G * BLOCK), jnp.float32),
        ),
        compiler_params=pltpu.CompilerParams(vmem_limit_bytes=32 * 1024 * 1024),
        name="attend" if fast else "attend_gathered",
    )(where, wanted, info, query, key_run, value_run, pool, query_pool)


SHARE = HEADS * WIDTH // RUNS


def merge_kernel(part, stats, merged, got, got_stats, piece, send, land, send_stats, land_stats, back, home):
    me = lax.axis_index("seq")
    peers = [lax.rem(me + k, RUNS) for k in range(1, RUNS)]
    greet([place(peer) for peer in peers])

    def rows(who):
        return who // 4, pl.ds(lax.rem(who, 4) * SHARE, SHARE)

    def hand(k, slot):
        to = lax.rem(me + k, RUNS)
        head, span = rows(to)
        weighted = pltpu.make_async_remote_copy(
            src_ref=part.at[head, span],
            dst_ref=got.at[slot],
            send_sem=send.at[k],
            recv_sem=land.at[k],
            device_id=place(to),
            device_id_type=MESH,
        )
        sums = pltpu.make_async_remote_copy(
            src_ref=stats.at[head],
            dst_ref=got_stats.at[slot],
            send_sem=send_stats.at[k],
            recv_sem=land_stats.at[k],
            device_id=place(to),
            device_id_type=MESH,
        )
        return weighted, sums

    def give(k, who):
        head, span = rows(who)
        return pltpu.make_async_remote_copy(
            src_ref=piece,
            dst_ref=merged.at[head, span],
            send_sem=back.at[k],
            recv_sem=home.at[k],
            device_id=place(lax.rem(me + k, RUNS)),
            device_id_type=MESH,
        )

    for k in range(1, RUNS):
        for copy in hand(k, me):
            copy.start()
    head, span = rows(me)
    got[me] = part[head, span]
    got_stats[me] = stats[head]
    for k in range(1, RUNS):
        for copy in hand(k, lax.rem(me + RUNS - k, RUNS)):
            copy.wait_recv()
    peaks = got_stats[:, 0, :]
    weights = got_stats[:, 1, :] * jnp.exp(peaks - jnp.max(peaks, axis=0, keepdims=True))
    weights = weights / jnp.sum(weights, axis=0, keepdims=True)
    total = jnp.zeros((SHARE, G * BLOCK), jnp.float32)
    for device in range(RUNS):
        total = total + weights[device : device + 1, :] * got[device].astype(jnp.float32)
    piece[...] = total.astype(jnp.bfloat16)
    for k in range(1, RUNS):
        give(k, me).start()
    merged[head, span] = piece[...]
    for k in range(1, RUNS):
        for copy in hand(k, me):
            copy.wait_send()
        give(k, me).wait_send()
        give(k, lax.rem(me + RUNS - k, RUNS)).wait_recv()


def merge(part, stats):
    dma = pltpu.SemaphoreType.DMA
    vmem = pl.BlockSpec(memory_space=pltpu.VMEM)
    return pl.pallas_call(
        merge_kernel,
        in_specs=[vmem, vmem],
        out_specs=vmem,
        out_shape=jax.ShapeDtypeStruct((HEADS, WIDTH, G * BLOCK), jnp.bfloat16),
        scratch_shapes=[
            pltpu.VMEM((RUNS, SHARE, G * BLOCK), jnp.bfloat16),
            pltpu.VMEM((RUNS, 8, G * BLOCK), jnp.float32),
            pltpu.VMEM((SHARE, G * BLOCK), jnp.bfloat16),
        ]
        + [dma((RUNS,))] * 6,
        compiler_params=pltpu.CompilerParams(collective_id=2, has_side_effects=True),
        name="merge",
    )(part, stats)


def with_halo(block, width):
    count = lax.axis_size("seq")
    forward = [(i, i + 1) for i in range(count - 1)]
    backward = [(target, source) for source, target in forward]
    low = lax.ppermute(block[:, :, -width:], "seq", forward)
    high = lax.ppermute(block[:, :, :width], "seq", backward)
    return jnp.concatenate([low, block, high], axis=2)


def local(queries, keys, values, window_radius, global_ids, rand_owner, rand_local):
    shards = lax.axis_size("seq")
    position = lax.axis_index("seq")
    block_ids = position * NB_DEV + jnp.arange(NB_DEV, dtype=jnp.int32)

    by_head = jnp.stack((keys, values)).transpose(0, 2, 1, 3)
    pairs = by_head.reshape(2, HEADS, NB_DEV, BLOCK, WIDTH).transpose(1, 2, 0, 3, 4)
    pairs = pairs.reshape((OWN,) + UNIT)
    query_heads = queries.transpose(1, 0, 2)
    query_blocks = query_heads.reshape(HEADS, NB_DEV, BLOCK, WIDTH)
    units = jnp.concatenate(
        [
            lax.dynamic_index_in_dim(query_blocks, global_ids[g] % NB_DEV, axis=1, keepdims=False)
            for g in range(G)
        ]
    ).reshape((QUNITS,) + UNIT)
    wanted = (rand_owner[0] * NB_DEV + rand_local[0]).astype(jnp.int32)
    wanted = wanted.transpose(1, 0, 2).reshape(HEADS, PICKS)
    table, pool = exchange(jnp.pad(wanted, ((0, 0), (0, WIDTH - PICKS))), pairs, units)
    source, where, rest = plan(table, global_ids)
    log, flag = packets(source, pool, rest)

    runs = with_halo(by_head, WIN * BLOCK)
    info = jnp.concatenate(
        (window_radius, jnp.stack((position * NB_DEV, jnp.int32(shards * NB_DEV))), global_ids)
    ).astype(jnp.int32)
    rest_args = (where, wanted.reshape(-1), info, query_heads, runs[0], runs[1])

    def from_packets(pairs, units, log):
        return attend(True, *rest_args, log, log)

    def from_gather(pairs, units, log):
        everything = lax.all_gather(pairs, "seq", axis=0, tiled=True)
        holder = jnp.repeat(global_ids // NB_DEV, QUNITS // G) == position
        asked = lax.psum(jnp.where(holder[:, None, None, None], units, 0), "seq")
        return attend(False, *rest_args, everything, asked)

    sparse, part, stats = lax.cond(
        jnp.max(flag) > 0, from_gather, from_packets, pairs, units, log
    )
    global_out = merge(part, stats).reshape(HEADS, WIDTH, G, BLOCK).transpose(2, 3, 0, 1)

    result = sparse.reshape(HEADS, NB_DEV, BLOCK, WIDTH).transpose(1, 2, 0, 3)
    for slot in range(G):
        owned = global_ids[slot] == block_ids
        result = jnp.where(owned[:, None, None, None], global_out[slot][None], result)
    return result.reshape(NB_DEV * BLOCK, HEADS, WIDTH)


def solution(mesh):
    placed = (
        P(("dp", "seq"), "tensor", None),
        P(("dp", "seq"), "tensor", None),
        P(("dp", "seq"), "tensor", None),
        P(("dp", "tensor")),
        P("dp"),
        P("tensor", ("dp", "seq"), None, None),
        P("tensor", ("dp", "seq"), None, None),
    )
    return jax.shard_map(
        local,
        mesh=mesh,
        in_specs=placed,
        out_specs=P(("dp", "seq"), "tensor", None),
        check_vma=False,
    )
```

```python
import math

import jax
import jax.numpy as jnp
from jax import lax
from jax.experimental import pallas as pl
from jax.experimental.pallas import tpu as pltpu
from jax.sharding import PartitionSpec as P

BLOCK = 64
WIN = 3
G = 2
R = 3
NB_DEV = 8
HEADS = 8
WIDTH = 128
WKEYS = (2 * WIN + 1) * BLOCK
PICKS = NB_DEV * R
NEAR = NB_DEV + 2 * WIN
FETCH = NEAR + G + PICKS

RUNS = 32
CHIPS = 16
CODES = RUNS * NB_DEV
OWN = HEADS * NB_DEV
QUNITS = 8
UNITS = 2 * QUNITS + 2 * OWN
SLOTS = 8
PHASES = 37
PIECES = 4
PIECE = SLOTS // PIECES
STAGES = 4
ENTRIES = 2 * PHASES * 2 * SLOTS
UNIT = (2, BLOCK, WIDTH)
MESH = pl.DeviceIdType.MESH


def place(seq):
    return (lax.axis_index("dp"), seq, lax.axis_index("tensor"))


def greet(devices):
    barrier = pltpu.get_barrier_semaphore()
    for device in devices:
        pl.semaphore_signal(barrier, inc=1, device_id=device, device_id_type=MESH)
    pl.semaphore_wait(barrier, len(devices))


def exchange_kernel(wanted, pairs, units, table, pool, send, land, kept_sem, pair_send, pair_land):
    me = lax.axis_index("seq")
    side = lax.rem(me, 2)
    greet([place(lax.rem(me + k, RUNS)) for k in range(1, RUNS)])
    parts = (
        (units, lambda who: pool.at[pl.ds(who * QUNITS, QUNITS)]),
        (pairs, lambda who: pool.at[pl.ds(2 * QUNITS + who * OWN, OWN)]),
    )

    def across(i, who):
        return pltpu.make_async_remote_copy(
            src_ref=parts[i][0],
            dst_ref=parts[i][1](who),
            send_sem=pair_send.at[i],
            recv_sem=pair_land.at[i],
            device_id=place(me + 1 - 2 * side),
            device_id_type=MESH,
        )

    def tell(k, slot):
        return pltpu.make_async_remote_copy(
            src_ref=wanted,
            dst_ref=table.at[slot],
            send_sem=send.at[k],
            recv_sem=land.at[k],
            device_id=place(lax.rem(me + k, RUNS)),
            device_id_type=MESH,
        )

    for k in range(1, RUNS):
        tell(k, me).start()
    kept = [pltpu.make_async_copy(wanted, table.at[me], kept_sem.at[2])]
    for i in range(2):
        across(i, side).start()
        kept.append(pltpu.make_async_copy(parts[i][0], parts[i][1](side), kept_sem.at[i]))
    for copy in kept:
        copy.start()
    for k in range(1, RUNS):
        tell(k, me).wait_send()
        tell(k, lax.rem(me + RUNS - k, RUNS)).wait_recv()
    for i in range(2):
        across(i, side).wait_send()
        across(i, 1 - side).wait_recv()
    for copy in kept:
        copy.wait()


def exchange(wanted, pairs, units):
    dma = pltpu.SemaphoreType.DMA
    vmem = pl.BlockSpec(memory_space=pltpu.VMEM)
    hbm = pl.BlockSpec(memory_space=pl.ANY)
    return pl.pallas_call(
        exchange_kernel,
        in_specs=[vmem, hbm, hbm],
        out_specs=(vmem, hbm),
        out_shape=(
            jax.ShapeDtypeStruct((RUNS, HEADS, WIDTH), jnp.int32),
            jax.ShapeDtypeStruct((UNITS,) + UNIT, jnp.bfloat16),
        ),
        scratch_shapes=[dma((RUNS,)), dma((RUNS,)), dma((3,)), dma((2,)), dma((2,))],
        compiler_params=pltpu.CompilerParams(collective_id=0, has_side_effects=True),
        name="exchange",
    )(wanted, pairs, units)


def plan_kernel(global_ids, table, radius, source, where, rest, keys, numbers, sems):
    me = lax.axis_index("seq")
    chip, side = me // 2, lax.rem(me, 2)
    shape = (HEADS, CODES)
    code = lax.broadcasted_iota(jnp.int32, shape, 1)
    row = lax.broadcasted_iota(jnp.int32, shape, 0)
    home = code >> 4
    first, second = global_ids[0], global_ids[1]
    everywhere = ((code == first) | (code == second)).astype(jnp.int32)

    def reaches(d, state):
        right, left, far = state
        picked = table[d]
        apart = code - d * NB_DEV
        beside = (apart >= -radius[...]) & (apart < NB_DEV + radius[...])
        hit = everywhere | beside.astype(jnp.int32)
        for k in range(PICKS):
            hit = hit | (picked[:, k : k + 1] == code).astype(jnp.int32)
        delta = ((d >> 1) - home) & (CHIPS - 1)
        right = jnp.maximum(right, jnp.where(delta < 8, hit * delta, 0))
        left = jnp.maximum(left, jnp.where(delta > 8, hit * (CHIPS - delta), 0))
        return right, left, far | jnp.where(delta == 8, hit, 0)

    zero = jnp.zeros(shape, jnp.int32)
    right, left, far = lax.fori_loop(0, RUNS, reaches, (zero, zero, zero))
    by_right = (right > left) | ((right == left) & (((row + code) & 1) == 0))
    right = jnp.where((far > 0) & by_right, 8, right)
    left = jnp.where((far > 0) & ~by_right, 8, left)

    lane_i = lax.broadcasted_iota(jnp.int32, (CODES, CODES), 0)
    lane_j = lax.broadcasted_iota(jnp.int32, (CODES, CODES), 1)
    together = (lane_i >> 4) == (lane_j >> 4)
    group = together.astype(jnp.bfloat16)
    before = (together & (lane_i < lane_j)).astype(jnp.bfloat16)
    holds_first = (home == (first >> 4)).astype(jnp.int32)
    holds_second = (home == (second >> 4)).astype(jnp.int32)
    asked = (holds_first + holds_second) * (QUNITS // G)

    def running_rows(x):
        height = x.shape[0]
        line = lax.broadcasted_iota(jnp.int32, x.shape, 0)
        step = 1
        while step < height:
            x = x + jnp.where(line >= step, pltpu.roll(x, step, 0), 0)
            step *= 2
        return x

    def last_row(x):
        return jnp.broadcast_to(x[x.shape[0] - 1 :, :], x.shape)

    def order(extent):
        rank = jnp.full(shape, 4096, jnp.int32)
        reach = [None] * 9
        above = asked
        for p in range(8, 0, -1):
            same = (extent == p).astype(jnp.bfloat16)
            in_group = jnp.dot(same, group, preferred_element_type=jnp.float32).astype(jnp.int32)
            ahead = jnp.dot(same, before, preferred_element_type=jnp.float32).astype(jnp.int32)
            running = running_rows(in_group)
            rank = jnp.where(extent == p, above + running - in_group + ahead, rank)
            above = above + last_row(running)
            reach[p] = above
        return rank, reach

    ways = [order(extent) for extent in (right, left)]
    wide = lambda x: jnp.concatenate((x, x), axis=0)
    reaches_wide = [[None] + [wide(x) for x in reach[1:]] for rank, reach in ways]

    def phase(t, state):
        after = []
        for way in range(2):
            rank, reach = ways[way][0], reaches_wide[way]
            going, queue, start, slot = state[4 * way : 4 * way + 4]
            free = (going == 0).astype(jnp.int32)
            running = running_rows(free)
            nth = running - free
            number = queue + nth
            fresh = (free > 0) & (number < reach[1])
            extent = sum((number < reach[p]).astype(jnp.int32) for p in range(1, 9))
            going = jnp.where(fresh, extent, going)
            taken = jnp.minimum(queue + last_row(running), reach[1])
            mark = jnp.where(fresh, number, -1)
            for s in range(2 * SLOTS):
                here = rank == jnp.broadcast_to(mark[s : s + 1, :], shape)
                start = jnp.where(here, t, start)
                slot = jnp.where(here, s, slot)
            going = jnp.maximum(pltpu.roll(going, 16 if way == 0 else CODES - 16, 1) - 1, 0)
            after += [going, taken, start, slot]
        return tuple(after)

    state = lax.fori_loop(0, PHASES, phase, (wide(zero), wide(zero), zero, zero) * 2)
    over = wide(zero)
    for way in range(2):
        over = over + state[4 * way] + reaches_wide[way][1] - state[4 * way + 1]
    over = over[:HEADS] + over[HEADS:]
    rest[...] = over[:, :128] + over[:, 128:]

    delta = (chip - home) & (CHIPS - 1)
    core = (code >> 3) & 1
    near = ENTRIES + 2 * QUNITS + core * OWN + row * NB_DEV + (code & 7)
    goes = [state[2] + delta - 1, PHASES + state[6] + CHIPS - delta - 1]
    slots = [state[3], state[7]]
    entry = [(goes[way] * 2 + (slots[way] & 1)) * SLOTS + (slots[way] >> 1) for way in range(2)]
    from_left = (delta < 8) | ((delta == 8) & (right == 8))
    far_entry = jnp.clip(jnp.where(from_left, entry[0], entry[1]), 0, ENTRIES - 1)
    where[...] = jnp.where(delta == 0, near, far_entry)

    for way in range(2):
        rank, reach = ways[way]
        sent = rank < state[4 * way + 1][:HEADS]
        keys[way] = jnp.where(sent, state[4 * way + 2] * 2 * SLOTS + state[4 * way + 3], -1)
    fetch = pltpu.make_async_copy(keys, numbers, sems)
    fetch.start()
    fetch.wait()

    def clear(i, carry):
        source[i] = -1
        return carry

    lax.fori_loop(0, 2 * PHASES * SLOTS, clear, 0, unroll=8)
    base = chip * 2 * NB_DEV
    has = [chip == (first >> 4), chip == (second >> 4)]
    count = (has[0].astype(jnp.int32) + has[1].astype(jnp.int32)) * (QUNITS // G)
    for way in range(2):

        def put(i, carry):
            lane = i & 15
            key = numbers[way, i >> 4, base + lane]

            @pl.when((key >= 0) & ((key & 1) == side))
            def _():
                unit = 2 * QUNITS + (lane >> 3) * OWN + (i >> 4) * NB_DEV + (lane & 7)
                source[way * PHASES * SLOTS + (key >> 1)] = unit

            return carry

        lax.fori_loop(0, 2 * OWN, put, 0, unroll=4)
        for r in range(QUNITS):
            late = jnp.logical_not(has[0]) if r < QUNITS // G else True
            late = jnp.asarray(late)
            core = (jnp.where(late, second, first) >> 3) & 1
            unit = core * QUNITS + jnp.where(late, QUNITS // G, 0) + r % (QUNITS // G)

            @pl.when((r < count) & (side == r % 2))
            def _():
                source[way * PHASES * SLOTS + r // 2] = unit


def plan(global_ids, table, radius):
    vmem = pl.BlockSpec(memory_space=pltpu.VMEM)
    smem = pl.BlockSpec(memory_space=pltpu.SMEM)
    return pl.pallas_call(
        plan_kernel,
        in_specs=[smem, vmem, vmem],
        out_specs=(smem, vmem, vmem),
        out_shape=(
            jax.ShapeDtypeStruct((2 * PHASES * SLOTS,), jnp.int32),
            jax.ShapeDtypeStruct((HEADS, CODES), jnp.int32),
            jax.ShapeDtypeStruct((HEADS, 128), jnp.int32),
        ),
        scratch_shapes=[
            pltpu.VMEM((2, HEADS, CODES), jnp.int32),
            pltpu.SMEM((2, HEADS, CODES), jnp.int32),
            pltpu.SemaphoreType.DMA(()),
        ],
        name="plan",
    )(global_ids, table, radius)


def packet_kernel(
    source, pool, rest, log, flag, recv, stage, votes,
    send_sem, land_sem, keep_sem, across_sem, across_land, tail_sem, vote_send, vote_land,
):
    me = lax.axis_index("seq")
    chip, side = me // 2, lax.rem(me, 2)
    sibling = me + 1 - 2 * side
    ahead = lax.rem(chip + 1, CHIPS) * 2 + side
    behind = lax.rem(chip + CHIPS - 1, CHIPS) * 2 + side
    dp, tensor = lax.axis_index("dp"), lax.axis_index("tensor")
    ring = dp * 8 + tensor

    def other(k):
        there = lax.rem(ring + k, 16)
        return (there // 8, me, lax.rem(there, 8))

    greet([place(ahead), place(behind), place(sibling)] + [other(k) for k in range(1, 16)])

    def vote(k, slot):
        return pltpu.make_async_remote_copy(
            src_ref=rest,
            dst_ref=votes.at[slot],
            send_sem=vote_send.at[k],
            recv_sem=vote_land.at[k],
            device_id=other(k),
            device_id_type=MESH,
        )

    for k in range(1, 16):
        vote(k, ring).start()
    kept = pltpu.make_async_copy(pool, log.at[pl.ds(ENTRIES, UNITS)], tail_sem.at[0])
    kept.start()
    own_vote = pltpu.make_async_copy(rest, votes.at[ring], tail_sem.at[1])
    own_vote.start()

    def hop(t, way, piece):
        rows = pl.ds(piece * PIECE, PIECE)
        return pltpu.make_async_remote_copy(
            src_ref=stage.at[way, lax.rem(t, STAGES), rows],
            dst_ref=recv.at[way, t, rows],
            send_sem=send_sem.at[way, lax.rem(t, STAGES), piece],
            recv_sem=land_sem.at[way, t, piece],
            device_id=place(ahead if way == 0 else behind),
            device_id_type=MESH,
        )

    def entry(t, way, who):
        return pl.ds(((way * PHASES + t) * 2 + who) * SLOTS, SLOTS)

    def keep(t, way):
        return pltpu.make_async_copy(
            recv.at[way, t], log.at[entry(t, way, side)], keep_sem.at[way, lax.rem(t, 2)]
        )

    def across(t, way, who):
        return pltpu.make_async_remote_copy(
            src_ref=recv.at[way, t],
            dst_ref=log.at[entry(t, way, who)],
            send_sem=across_sem.at[way, lax.rem(t, 2)],
            recv_sem=across_land.at[way, t],
            device_id=place(sibling),
            device_id_type=MESH,
        )

    def compose(t, way, piece, first):
        for i in range(PIECE):
            slot = piece * PIECE + i
            wanted = source[(way * PHASES + t) * SLOTS + slot]
            unit = pool[jnp.maximum(wanted, 0)]
            if not first:
                unit = jnp.where(wanted >= 0, unit, recv[way, t - 1, slot])
            stage[way, lax.rem(t, STAGES), slot] = unit

    for piece in range(PIECES):
        for way in range(2):
            compose(0, way, piece, True)
            hop(0, way, piece).start()

    def settle(t):
        for way in range(2):
            keep(t, way).wait()
            across(t, way, side).wait_send()

    def pass_on(t):
        pl.when(t >= 2)(lambda: settle(t - 2))
        for way in range(2):
            keep(t, way).start()
            across(t, way, side).start()

    def phase(t, carry):
        def step(piece, inner):
            for way in range(2):
                hop(t - 1, way, piece).wait_recv()
                pl.when(t >= STAGES)(lambda: hop(t - STAGES, way, piece).wait_send())
                compose(t, way, piece, False)
                hop(t, way, piece).start()
            return inner

        lax.fori_loop(0, PIECES, step, 0, unroll=True)
        pass_on(t - 1)
        return carry

    lax.fori_loop(1, PHASES, phase, 0)

    def last(piece, carry):
        for way in range(2):
            hop(PHASES - 1, way, piece).wait_recv()
            for t in range(PHASES - STAGES, PHASES):
                hop(t, way, piece).wait_send()
        return carry

    lax.fori_loop(0, PIECES, last, 0)
    pass_on(PHASES - 1)
    settle(PHASES - 2)
    settle(PHASES - 1)

    def drain(t, carry):
        for way in range(2):
            across(t, way, 1 - side).wait_recv()
        return carry

    lax.fori_loop(0, PHASES, drain, 0)
    for k in range(1, 16):
        vote(k, ring).wait_send()
        vote(k, lax.rem(ring + 16 - k, 16)).wait_recv()
    kept.wait()
    own_vote.wait()
    flag[...] = jnp.max(votes[...], axis=0)


def packets(source, pool, rest):
    dma = pltpu.SemaphoreType.DMA
    vmem = pl.BlockSpec(memory_space=pltpu.VMEM)
    return pl.pallas_call(
        packet_kernel,
        in_specs=[
            pl.BlockSpec(memory_space=pltpu.SMEM),
            vmem,
            vmem,
        ],
        out_specs=(pl.BlockSpec(memory_space=pl.ANY), vmem),
        out_shape=(
            jax.ShapeDtypeStruct((ENTRIES + UNITS,) + UNIT, jnp.bfloat16),
            jax.ShapeDtypeStruct((HEADS, 128), jnp.int32),
        ),
        scratch_shapes=[
            pltpu.VMEM((2, PHASES, SLOTS) + UNIT, jnp.bfloat16),
            pltpu.VMEM((2, STAGES, SLOTS) + UNIT, jnp.bfloat16),
            pltpu.VMEM((16, HEADS, 128), jnp.int32),
            dma((2, STAGES, PIECES)),
            dma((2, PHASES, PIECES)),
            dma((2, 2)),
            dma((2, 2)),
            dma((2, PHASES)),
            dma((2,)),
            dma((16,)),
            dma((16,)),
        ],
        compiler_params=pltpu.CompilerParams(
            collective_id=1, has_side_effects=True, vmem_limit_bytes=48 * 1024 * 1024
        ),
        name="packets",
    )(source, pool, rest)


def attend_kernel(
    fast, where, wanted, info, query, pool, query_pool, out, part, stats,
    fetched, asked, sems, asked_sems,
):
    head = pl.program_id(0)
    first = info[HEADS]

    def spot(code, h):
        if fast:
            return where[h, code]
        return (code >> 3) * OWN + h * NB_DEV + (code & 7)

    def query_spot(g, h):
        unit = g * (QUNITS // G) + h // 2
        if not fast:
            return unit
        mine = first >> 3
        owner = info[HEADS + 1 + g] >> 3
        core = owner & 1
        delta = ((mine >> 1) - (owner >> 1)) & (CHIPS - 1)
        shared = (owner >> 1) == (info[HEADS + 1] >> 4)
        rank = jnp.where(shared, unit, h // 2)
        near = ENTRIES + core * QUNITS + unit
        step = jnp.where(delta <= 8, delta - 1, PHASES + CHIPS - delta - 1)
        far = (step * 2 + (rank & 1)) * SLOTS + (rank >> 1)
        return jnp.where(delta == 0, near, far)

    def copies(h, slot):
        for i in range(FETCH):
            if i < NEAR:
                code = jnp.clip(first - WIN + i, 0, CODES - 1)
            elif i < NEAR + G:
                code = info[HEADS + 1 + i - NEAR]
            else:
                code = wanted[h * PICKS + i - NEAR - G]
            yield pltpu.make_async_copy(
                pool.at[spot(code, h)], fetched.at[slot, i], sems.at[slot, i]
            )
        for g in range(G):
            yield pltpu.make_async_copy(
                query_pool.at[query_spot(g, h), h % 2], asked.at[slot, g], asked_sems.at[slot, g]
            )

    @pl.when(head == 0)
    def _():
        for copy in copies(head, 0):
            copy.start()

    @pl.when(head + 1 < HEADS)
    def _():
        for copy in copies(head + 1, (head + 1) % 2):
            copy.start()

    slot = head % 2
    for copy in copies(head, slot):
        copy.wait()
    radius = info[head]
    column = lax.broadcasted_iota(jnp.int32, (1, WKEYS), 1) // BLOCK - WIN
    contract = (((1,), (1,)), ((), ()))
    scale = 1.0 / math.sqrt(WIDTH)

    own = range(WIN, WIN + NB_DEV)
    scores = scale * lax.dot_general(
        jnp.concatenate([fetched[slot, i, 0] for i in own], axis=0),
        asked[slot].reshape(G * BLOCK, WIDTH),
        contract,
        preferred_element_type=jnp.float32,
    )
    peak = jnp.max(scores, axis=0, keepdims=True)
    weights = jnp.exp(scores - peak)
    sums = jnp.sum(weights, axis=0, keepdims=True)
    weighted = lax.dot_general(
        jnp.concatenate([fetched[slot, i, 1] for i in own], axis=0),
        weights.astype(jnp.bfloat16),
        (((0,), (0,)), ((), ())),
        preferred_element_type=jnp.float32,
    )
    part[0] = (weighted / sums).astype(jnp.bfloat16)
    stats[0] = jnp.concatenate((peak, sums, jnp.zeros((6, WIDTH), jnp.float32)), axis=0)

    def one_block(b, carry):
        rows = pl.ds(pl.multiple_of(b * BLOCK, BLOCK), BLOCK)
        q = query[0, rows]
        window = [b + i for i in range(2 * WIN + 1)]
        near_keys = jnp.concatenate([fetched[slot, i, 0] for i in window], axis=0)
        near_values = jnp.concatenate([fetched[slot, i, 1] for i in window], axis=0)
        others = [NEAR, NEAR + 1] + [NEAR + G + b * R + r for r in range(R)]
        far_keys = jnp.concatenate([fetched[slot, i, 0] for i in others], axis=0)
        far_values = jnp.concatenate([fetched[slot, i, 1] for i in others], axis=0)
        target = first + b + column
        usable = (jnp.abs(column) <= radius) & (target >= 0) & (target < CODES)
        near = lax.dot_general(q, near_keys, contract, preferred_element_type=jnp.float32)
        near = jnp.where(usable, near * scale, -jnp.inf)
        far = lax.dot_general(q, far_keys, contract, preferred_element_type=jnp.float32) * scale
        peak = jnp.maximum(
            jnp.max(near, axis=1, keepdims=True), jnp.max(far, axis=1, keepdims=True)
        )
        near = jnp.exp(near - peak)
        far = jnp.exp(far - peak)
        row_total = jnp.sum(near, axis=1, keepdims=True) + jnp.sum(far, axis=1, keepdims=True)
        weighted = jnp.dot(
            near.astype(jnp.bfloat16), near_values, preferred_element_type=jnp.float32
        ) + jnp.dot(far.astype(jnp.bfloat16), far_values, preferred_element_type=jnp.float32)
        out[0, rows] = (weighted / row_total).astype(jnp.bfloat16)
        return carry

    lax.fori_loop(0, NB_DEV, one_block, 0, unroll=2)


def attend(fast, where, wanted, info, query, pool, query_pool):
    per_head = lambda rows: pl.BlockSpec((1, rows, WIDTH), lambda h, *_: (h, 0, 0))
    return pl.pallas_call(
        lambda *refs: attend_kernel(fast, *refs),
        grid_spec=pltpu.PrefetchScalarGridSpec(
            num_scalar_prefetch=3,
            grid=(HEADS,),
            in_specs=[
                per_head(NB_DEV * BLOCK),
                pl.BlockSpec(memory_space=pl.ANY),
                pl.BlockSpec(memory_space=pl.ANY),
            ],
            out_specs=(per_head(NB_DEV * BLOCK), per_head(WIDTH), per_head(8)),
            scratch_shapes=[
                pltpu.VMEM((2, FETCH) + UNIT, jnp.bfloat16),
                pltpu.VMEM((2, G, BLOCK, WIDTH), jnp.bfloat16),
                pltpu.SemaphoreType.DMA((2, FETCH)),
                pltpu.SemaphoreType.DMA((2, G)),
            ],
        ),
        out_shape=(
            jax.ShapeDtypeStruct((HEADS, NB_DEV * BLOCK, WIDTH), jnp.bfloat16),
            jax.ShapeDtypeStruct((HEADS, WIDTH, G * BLOCK), jnp.bfloat16),
            jax.ShapeDtypeStruct((HEADS, 8, G * BLOCK), jnp.float32),
        ),
        compiler_params=pltpu.CompilerParams(vmem_limit_bytes=32 * 1024 * 1024),
        name="attend" if fast else "attend_gathered",
    )(where, wanted, info, query, pool, query_pool)


HALF = HEADS // 2
SHARE = HALF * WIDTH // CHIPS


def merge_kernel(
    part, stats, merged, theirs, their_stats, half, half_stats, got, got_stats, piece,
    pair_send, pair_land, send, land, send_stats, land_stats, back, home,
):
    me = lax.axis_index("seq")
    chip, side = me // 2, lax.rem(me, 2)
    sibling = me + 1 - 2 * side
    peers = [lax.rem(chip + k, CHIPS) * 2 + side for k in range(1, CHIPS)]
    greet([place(peer) for peer in peers] + [place(sibling)])

    def pair(i, source, target):
        return pltpu.make_async_remote_copy(
            src_ref=source,
            dst_ref=target,
            send_sem=pair_send.at[i],
            recv_sem=pair_land.at[i],
            device_id=place(sibling),
            device_id_type=MESH,
        )

    their_heads = pl.ds((1 - side) * HALF, HALF)
    my_heads = pl.ds(side * HALF, HALF)
    swaps = [
        pair(0, part.at[their_heads], theirs),
        pair(1, stats.at[their_heads], their_stats),
    ]
    for copy in swaps:
        copy.start()
    for copy in swaps:
        copy.wait_recv()
    for h in range(HALF):
        mine = stats[side * HALF + h]
        other = their_stats[h]
        peak = jnp.maximum(mine[0:1, :], other[0:1, :])
        first = mine[1:2, :] * jnp.exp(mine[0:1, :] - peak)
        second = other[1:2, :] * jnp.exp(other[0:1, :] - peak)
        total = first + second
        weighted = (first / total) * part[side * HALF + h].astype(jnp.float32) + (
            second / total
        ) * theirs[h].astype(jnp.float32)
        half[h] = weighted.astype(jnp.bfloat16)
        half_stats[h : h + 1, :] = peak
        half_stats[HALF + h : HALF + h + 1, :] = total

    def rows(who):
        return who // 4, pl.ds(lax.rem(who, 4) * SHARE, SHARE)

    def hand(k, slot):
        to = lax.rem(chip + k, CHIPS)
        head, span = rows(to)
        weighted = pltpu.make_async_remote_copy(
            src_ref=half.at[head, span],
            dst_ref=got.at[slot],
            send_sem=send.at[k],
            recv_sem=land.at[k],
            device_id=place(to * 2 + side),
            device_id_type=MESH,
        )
        sums = pltpu.make_async_remote_copy(
            src_ref=half_stats,
            dst_ref=got_stats.at[slot],
            send_sem=send_stats.at[k],
            recv_sem=land_stats.at[k],
            device_id=place(to * 2 + side),
            device_id_type=MESH,
        )
        return weighted, sums

    def give(k, who):
        head, span = rows(who)
        return pltpu.make_async_remote_copy(
            src_ref=piece,
            dst_ref=merged.at[side * HALF + head, span],
            send_sem=back.at[k],
            recv_sem=home.at[k],
            device_id=place(lax.rem(chip + k, CHIPS) * 2 + side),
            device_id_type=MESH,
        )

    for k in range(1, CHIPS):
        for copy in hand(k, chip):
            copy.start()
    head, span = rows(chip)
    got[chip] = half[head, span]
    got_stats[chip] = half_stats[...]
    for k in range(1, CHIPS):
        for copy in hand(k, lax.rem(chip + CHIPS - k, CHIPS)):
            copy.wait_recv()
    all_stats = got_stats[...]
    peaks = jnp.zeros((CHIPS, G * BLOCK), jnp.float32)
    sums = jnp.zeros((CHIPS, G * BLOCK), jnp.float32)
    for h in range(HALF):
        peaks = jnp.where(head == h, all_stats[:, h, :], peaks)
        sums = jnp.where(head == h, all_stats[:, HALF + h, :], sums)
    weights = sums * jnp.exp(peaks - jnp.max(peaks, axis=0, keepdims=True))
    weights = weights / jnp.sum(weights, axis=0, keepdims=True)
    total = jnp.zeros((SHARE, G * BLOCK), jnp.float32)
    for k in range(CHIPS):
        total = total + weights[k : k + 1, :] * got[k].astype(jnp.float32)
    piece[...] = total.astype(jnp.bfloat16)
    for k in range(1, CHIPS):
        give(k, chip).start()
    merged[side * HALF + head, span] = piece[...]
    for k in range(1, CHIPS):
        give(k, lax.rem(chip + CHIPS - k, CHIPS)).wait_recv()
    last = pair(2, merged.at[my_heads], merged.at[my_heads])
    last.start()
    for copy in swaps:
        copy.wait_send()
    for k in range(1, CHIPS):
        for copy in hand(k, chip):
            copy.wait_send()
        give(k, chip).wait_send()
    last.wait_send()
    pair(2, merged.at[their_heads], merged.at[their_heads]).wait_recv()


def merge(part, stats):
    dma = pltpu.SemaphoreType.DMA
    vmem = pl.BlockSpec(memory_space=pltpu.VMEM)
    rows = G * BLOCK
    return pl.pallas_call(
        merge_kernel,
        in_specs=[vmem, vmem],
        out_specs=vmem,
        out_shape=jax.ShapeDtypeStruct((HEADS, WIDTH, rows), jnp.bfloat16),
        scratch_shapes=[
            pltpu.VMEM((HALF, WIDTH, rows), jnp.bfloat16),
            pltpu.VMEM((HALF, 8, rows), jnp.float32),
            pltpu.VMEM((HALF, WIDTH, rows), jnp.bfloat16),
            pltpu.VMEM((2 * HALF, rows), jnp.float32),
            pltpu.VMEM((CHIPS, SHARE, rows), jnp.bfloat16),
            pltpu.VMEM((CHIPS, 2 * HALF, rows), jnp.float32),
            pltpu.VMEM((SHARE, rows), jnp.bfloat16),
        ]
        + [dma((3,))] * 2
        + [dma((CHIPS,))] * 6,
        compiler_params=pltpu.CompilerParams(collective_id=2, has_side_effects=True),
        name="merge",
    )(part, stats)


def local(queries, keys, values, window_radius, global_ids, rand_owner, rand_local):
    position = lax.axis_index("seq")
    block_ids = position * NB_DEV + jnp.arange(NB_DEV, dtype=jnp.int32)

    pairs = jnp.stack((keys, values)).reshape(2, NB_DEV, BLOCK, HEADS, WIDTH)
    pairs = pairs.transpose(3, 1, 0, 2, 4).reshape((OWN,) + UNIT)
    query_heads = queries.transpose(1, 0, 2)
    query_blocks = query_heads.reshape(HEADS, NB_DEV, BLOCK, WIDTH)
    units = jnp.concatenate(
        [
            lax.dynamic_index_in_dim(query_blocks, global_ids[g] % NB_DEV, axis=1, keepdims=False)
            for g in range(G)
        ]
    ).reshape((QUNITS,) + UNIT)
    wanted = (rand_owner[0] * NB_DEV + rand_local[0]).astype(jnp.int32)
    wanted = wanted.transpose(1, 0, 2).reshape(HEADS, PICKS)
    table, pool = exchange(jnp.pad(wanted, ((0, 0), (0, WIDTH - PICKS))), pairs, units)
    radius = jnp.broadcast_to(window_radius[:, None], (HEADS, CODES)).astype(jnp.int32)
    source, where, rest = plan(global_ids, table, radius)
    log, flag = packets(source, pool, rest)
    info = jnp.concatenate((window_radius, (position * NB_DEV)[None], global_ids)).astype(jnp.int32)
    rest_args = (where, wanted.reshape(-1), info, query_heads)

    def from_packets(pairs, units, log):
        return attend(True, *rest_args, log, log)

    def from_gather(pairs, units, log):
        everything = lax.all_gather(pairs, "seq", axis=0, tiled=True)
        holder = jnp.repeat(global_ids // NB_DEV, QUNITS // G) == position
        asked = lax.psum(jnp.where(holder[:, None, None, None], units, 0), "seq")
        return attend(False, *rest_args, everything, asked)

    sparse, part, stats = lax.cond(
        jnp.max(flag) > 0, from_gather, from_packets, pairs, units, log
    )
    global_out = merge(part, stats).reshape(HEADS, WIDTH, G, BLOCK).transpose(2, 3, 0, 1)

    result = sparse.reshape(HEADS, NB_DEV, BLOCK, WIDTH).transpose(1, 2, 0, 3)
    for slot in range(G):
        owned = global_ids[slot] == block_ids
        result = jnp.where(owned[:, None, None, None], global_out[slot][None], result)
    return result.reshape(NB_DEV * BLOCK, HEADS, WIDTH)


def solution(mesh):
    placed = (
        P(("dp", "seq"), "tensor", None),
        P(("dp", "seq"), "tensor", None),
        P(("dp", "seq"), "tensor", None),
        P(("dp", "tensor")),
        P("dp"),
        P("tensor", ("dp", "seq"), None, None),
        P("tensor", ("dp", "seq"), None, None),
    )
    return jax.shard_map(
        local,
        mesh=mesh,
        in_specs=placed,
        out_specs=P(("dp", "seq"), "tensor", None),
        check_vma=False,
    )
```

```python
import math

import jax
import jax.numpy as jnp
from jax import lax
from jax.experimental import pallas as pl
from jax.experimental.pallas import tpu as pltpu
from jax.sharding import PartitionSpec as P

BLOCK = 64
WIN = 3
G = 2
R = 3
NB_DEV = 8
HEADS = 8
WIDTH = 128
WKEYS = (2 * WIN + 1) * BLOCK
PICKS = NB_DEV * R
NEAR = NB_DEV + 2 * WIN
FETCH = NEAR + G + PICKS

RUNS = 32
CHIPS = 16
CODES = RUNS * NB_DEV
OWN = HEADS * NB_DEV
QUNITS = 8
UNITS = 2 * QUNITS + 2 * OWN
SLOTS = 8
PHASES = 37
PIECES = 4
PIECE = SLOTS // PIECES
STAGES = 4
ENTRIES = 2 * PHASES * 2 * SLOTS
UNIT = (2, BLOCK, WIDTH)
MESH = pl.DeviceIdType.MESH


def place(seq):
    return (lax.axis_index("dp"), seq, lax.axis_index("tensor"))


def greet(devices):
    barrier = pltpu.get_barrier_semaphore()
    for device in devices:
        pl.semaphore_signal(barrier, inc=1, device_id=device, device_id_type=MESH)
    pl.semaphore_wait(barrier, len(devices))


def exchange_kernel(wanted, pairs, units, table, pool, send, land, kept_sem, pair_send, pair_land):
    me = lax.axis_index("seq")
    side = lax.rem(me, 2)
    greet([place(lax.rem(me + k, RUNS)) for k in range(1, RUNS)])
    parts = (
        (units, lambda who: pool.at[pl.ds(who * QUNITS, QUNITS)]),
        (pairs, lambda who: pool.at[pl.ds(2 * QUNITS + who * OWN, OWN)]),
    )

    def across(i, who):
        return pltpu.make_async_remote_copy(
            src_ref=parts[i][0],
            dst_ref=parts[i][1](who),
            send_sem=pair_send.at[i],
            recv_sem=pair_land.at[i],
            device_id=place(me + 1 - 2 * side),
            device_id_type=MESH,
        )

    def tell(k, slot):
        return pltpu.make_async_remote_copy(
            src_ref=wanted,
            dst_ref=table.at[slot],
            send_sem=send.at[k],
            recv_sem=land.at[k],
            device_id=place(lax.rem(me + k, RUNS)),
            device_id_type=MESH,
        )

    for k in range(1, RUNS):
        tell(k, me).start()
    kept = [pltpu.make_async_copy(wanted, table.at[me], kept_sem.at[2])]
    for i in range(2):
        across(i, side).start()
        kept.append(pltpu.make_async_copy(parts[i][0], parts[i][1](side), kept_sem.at[i]))
    for copy in kept:
        copy.start()
    for k in range(1, RUNS):
        tell(k, me).wait_send()
        tell(k, lax.rem(me + RUNS - k, RUNS)).wait_recv()
    for i in range(2):
        across(i, side).wait_send()
        across(i, 1 - side).wait_recv()
    for copy in kept:
        copy.wait()


def exchange(wanted, pairs, units):
    dma = pltpu.SemaphoreType.DMA
    vmem = pl.BlockSpec(memory_space=pltpu.VMEM)
    hbm = pl.BlockSpec(memory_space=pl.ANY)
    return pl.pallas_call(
        exchange_kernel,
        in_specs=[vmem, hbm, hbm],
        out_specs=(vmem, hbm),
        out_shape=(
            jax.ShapeDtypeStruct((RUNS, HEADS, WIDTH), jnp.int32),
            jax.ShapeDtypeStruct((UNITS,) + UNIT, jnp.bfloat16),
        ),
        scratch_shapes=[dma((RUNS,)), dma((RUNS,)), dma((3,)), dma((2,)), dma((2,))],
        compiler_params=pltpu.CompilerParams(collective_id=0, has_side_effects=True),
        name="exchange",
    )(wanted, pairs, units)


def plan_kernel(global_ids, table, radius, source, where, rest, keys, numbers, sems):
    me = lax.axis_index("seq")
    chip, side = me // 2, lax.rem(me, 2)
    shape = (HEADS, CODES)
    code = lax.broadcasted_iota(jnp.int32, shape, 1)
    row = lax.broadcasted_iota(jnp.int32, shape, 0)
    home = code >> 4
    first, second = global_ids[0], global_ids[1]
    everywhere = ((code == first) | (code == second)).astype(jnp.int32)

    def reaches(d, state):
        right, left, far = state
        picked = table[d]
        apart = code - d * NB_DEV
        beside = (apart >= -radius[...]) & (apart < NB_DEV + radius[...])
        hit = everywhere | beside.astype(jnp.int32)
        for k in range(PICKS):
            hit = hit | (picked[:, k : k + 1] == code).astype(jnp.int32)
        delta = ((d >> 1) - home) & (CHIPS - 1)
        right = jnp.maximum(right, jnp.where(delta < 8, hit * delta, 0))
        left = jnp.maximum(left, jnp.where(delta > 8, hit * (CHIPS - delta), 0))
        return right, left, far | jnp.where(delta == 8, hit, 0)

    zero = jnp.zeros(shape, jnp.int32)
    right, left, far = lax.fori_loop(0, RUNS, reaches, (zero, zero, zero))
    by_right = (right > left) | ((right == left) & (((row + code) & 1) == 0))
    right = jnp.where((far > 0) & by_right, 8, right)
    left = jnp.where((far > 0) & ~by_right, 8, left)

    lane_i = lax.broadcasted_iota(jnp.int32, (CODES, CODES), 0)
    lane_j = lax.broadcasted_iota(jnp.int32, (CODES, CODES), 1)
    together = (lane_i >> 4) == (lane_j >> 4)
    group = together.astype(jnp.bfloat16)
    before = (together & (lane_i < lane_j)).astype(jnp.bfloat16)
    holds_first = (home == (first >> 4)).astype(jnp.int32)
    holds_second = (home == (second >> 4)).astype(jnp.int32)
    asked = (holds_first + holds_second) * (QUNITS // G)

    def running_rows(x):
        height = x.shape[0]
        line = lax.broadcasted_iota(jnp.int32, x.shape, 0)
        step = 1
        while step < height:
            x = x + jnp.where(line >= step, pltpu.roll(x, step, 0), 0)
            step *= 2
        return x

    def last_row(x):
        return jnp.broadcast_to(x[x.shape[0] - 1 :, :], x.shape)

    def order(extent):
        rank = jnp.full(shape, 4096, jnp.int32)
        reach = [None] * 9
        above = asked
        for p in range(8, 0, -1):
            same = (extent == p).astype(jnp.bfloat16)
            in_group = jnp.dot(same, group, preferred_element_type=jnp.float32).astype(jnp.int32)
            ahead = jnp.dot(same, before, preferred_element_type=jnp.float32).astype(jnp.int32)
            running = running_rows(in_group)
            rank = jnp.where(extent == p, above + running - in_group + ahead, rank)
            above = above + last_row(running)
            reach[p] = above
        return rank, reach

    ways = [order(extent) for extent in (right, left)]
    wide = lambda x: jnp.concatenate((x, x), axis=0)
    reaches_wide = [[None] + [wide(x) for x in reach[1:]] for rank, reach in ways]

    def phase(t, state):
        after = []
        for way in range(2):
            rank, reach = ways[way][0], reaches_wide[way]
            going, queue, start, slot = state[4 * way : 4 * way + 4]
            free = (going == 0).astype(jnp.int32)
            running = running_rows(free)
            nth = running - free
            number = queue + nth
            fresh = (free > 0) & (number < reach[1])
            extent = sum((number < reach[p]).astype(jnp.int32) for p in range(1, 9))
            going = jnp.where(fresh, extent, going)
            taken = jnp.minimum(queue + last_row(running), reach[1])
            mark = jnp.where(fresh, number, -1)
            for s in range(2 * SLOTS):
                here = rank == jnp.broadcast_to(mark[s : s + 1, :], shape)
                start = jnp.where(here, t, start)
                slot = jnp.where(here, s, slot)
            going = jnp.maximum(pltpu.roll(going, 16 if way == 0 else CODES - 16, 1) - 1, 0)
            after += [going, taken, start, slot]
        return tuple(after)

    state = lax.fori_loop(0, PHASES, phase, (wide(zero), wide(zero), zero, zero) * 2)
    over = wide(zero)
    for way in range(2):
        over = over + state[4 * way] + reaches_wide[way][1] - state[4 * way + 1]
    over = over[:HEADS] + over[HEADS:]
    rest[...] = over[:, :128] + over[:, 128:]

    delta = (chip - home) & (CHIPS - 1)
    core = (code >> 3) & 1
    near = ENTRIES + 2 * QUNITS + core * OWN + row * NB_DEV + (code & 7)
    goes = [state[2] + delta - 1, PHASES + state[6] + CHIPS - delta - 1]
    slots = [state[3], state[7]]
    entry = [(goes[way] * 2 + (slots[way] & 1)) * SLOTS + (slots[way] >> 1) for way in range(2)]
    from_left = (delta < 8) | ((delta == 8) & (right == 8))
    far_entry = jnp.clip(jnp.where(from_left, entry[0], entry[1]), 0, ENTRIES - 1)
    where[...] = jnp.where(delta == 0, near, far_entry)

    for way in range(2):
        rank, reach = ways[way]
        sent = rank < state[4 * way + 1][:HEADS]
        keys[way] = jnp.where(sent, state[4 * way + 2] * 2 * SLOTS + state[4 * way + 3], -1)
    fetch = pltpu.make_async_copy(keys, numbers, sems)
    fetch.start()
    fetch.wait()

    def clear(i, carry):
        source[i] = -1
        return carry

    lax.fori_loop(0, 2 * PHASES * SLOTS, clear, 0, unroll=8)
    base = chip * 2 * NB_DEV
    has = [chip == (first >> 4), chip == (second >> 4)]
    count = (has[0].astype(jnp.int32) + has[1].astype(jnp.int32)) * (QUNITS // G)
    for way in range(2):

        def put(i, carry):
            lane = i & 15
            key = numbers[way, i >> 4, base + lane]

            @pl.when((key >= 0) & ((key & 1) == side))
            def _():
                unit = 2 * QUNITS + (lane >> 3) * OWN + (i >> 4) * NB_DEV + (lane & 7)
                source[way * PHASES * SLOTS + (key >> 1)] = unit

            return carry

        lax.fori_loop(0, 2 * OWN, put, 0, unroll=4)
        for r in range(QUNITS):
            late = jnp.logical_not(has[0]) if r < QUNITS // G else True
            late = jnp.asarray(late)
            core = (jnp.where(late, second, first) >> 3) & 1
            unit = core * QUNITS + jnp.where(late, QUNITS // G, 0) + r % (QUNITS // G)

            @pl.when((r < count) & (side == r % 2))
            def _():
                source[way * PHASES * SLOTS + r // 2] = unit


def plan(global_ids, table, radius):
    vmem = pl.BlockSpec(memory_space=pltpu.VMEM)
    smem = pl.BlockSpec(memory_space=pltpu.SMEM)
    return pl.pallas_call(
        plan_kernel,
        in_specs=[smem, vmem, vmem],
        out_specs=(smem, vmem, vmem),
        out_shape=(
            jax.ShapeDtypeStruct((2 * PHASES * SLOTS,), jnp.int32),
            jax.ShapeDtypeStruct((HEADS, CODES), jnp.int32),
            jax.ShapeDtypeStruct((HEADS, 128), jnp.int32),
        ),
        scratch_shapes=[
            pltpu.VMEM((2, HEADS, CODES), jnp.int32),
            pltpu.SMEM((2, HEADS, CODES), jnp.int32),
            pltpu.SemaphoreType.DMA(()),
        ],
        name="plan",
    )(global_ids, table, radius)


def packet_kernel(
    source, pool, rest, log, flag, recv, stage, votes,
    send_sem, land_sem, keep_sem, across_sem, across_land, tail_sem, vote_send, vote_land,
):
    me = lax.axis_index("seq")
    chip, side = me // 2, lax.rem(me, 2)
    sibling = me + 1 - 2 * side
    ahead = lax.rem(chip + 1, CHIPS) * 2 + side
    behind = lax.rem(chip + CHIPS - 1, CHIPS) * 2 + side
    dp, tensor = lax.axis_index("dp"), lax.axis_index("tensor")
    ring = dp * 8 + tensor

    def other(k):
        there = lax.rem(ring + k, 16)
        return (there // 8, me, lax.rem(there, 8))

    greet([place(ahead), place(behind), place(sibling)] + [other(k) for k in range(1, 16)])

    def vote(k, slot):
        return pltpu.make_async_remote_copy(
            src_ref=rest,
            dst_ref=votes.at[slot],
            send_sem=vote_send.at[k],
            recv_sem=vote_land.at[k],
            device_id=other(k),
            device_id_type=MESH,
        )

    for k in range(1, 16):
        vote(k, ring).start()
    kept = pltpu.make_async_copy(pool, log.at[pl.ds(ENTRIES, UNITS)], tail_sem.at[0])
    kept.start()
    own_vote = pltpu.make_async_copy(rest, votes.at[ring], tail_sem.at[1])
    own_vote.start()

    def hop(t, way, piece):
        rows = pl.ds(piece * PIECE, PIECE)
        return pltpu.make_async_remote_copy(
            src_ref=stage.at[way, lax.rem(t, STAGES), rows],
            dst_ref=recv.at[way, t, rows],
            send_sem=send_sem.at[way, lax.rem(t, STAGES), piece],
            recv_sem=land_sem.at[way, t, piece],
            device_id=place(ahead if way == 0 else behind),
            device_id_type=MESH,
        )

    def entry(t, way, who):
        return pl.ds(((way * PHASES + t) * 2 + who) * SLOTS, SLOTS)

    def keep(t, way):
        return pltpu.make_async_copy(
            recv.at[way, t], log.at[entry(t, way, side)], keep_sem.at[way, lax.rem(t, 2)]
        )

    def across(t, way, who):
        return pltpu.make_async_remote_copy(
            src_ref=recv.at[way, t],
            dst_ref=log.at[entry(t, way, who)],
            send_sem=across_sem.at[way, lax.rem(t, 2)],
            recv_sem=across_land.at[way, t],
            device_id=place(sibling),
            device_id_type=MESH,
        )

    def compose(t, way, piece, first):
        for i in range(PIECE):
            slot = piece * PIECE + i
            wanted = source[(way * PHASES + t) * SLOTS + slot]
            unit = pool[jnp.maximum(wanted, 0)]
            if not first:
                unit = jnp.where(wanted >= 0, unit, recv[way, t - 1, slot])
            stage[way, lax.rem(t, STAGES), slot] = unit

    for piece in range(PIECES):
        for way in range(2):
            compose(0, way, piece, True)
            hop(0, way, piece).start()

    def settle(t):
        for way in range(2):
            keep(t, way).wait()
            across(t, way, side).wait_send()

    def pass_on(t):
        pl.when(t >= 2)(lambda: settle(t - 2))
        for way in range(2):
            keep(t, way).start()
            across(t, way, side).start()

    def phase(t, carry):
        def step(piece, inner):
            for way in range(2):
                hop(t - 1, way, piece).wait_recv()
                pl.when(t >= STAGES)(lambda: hop(t - STAGES, way, piece).wait_send())
                compose(t, way, piece, False)
                hop(t, way, piece).start()
            return inner

        lax.fori_loop(0, PIECES, step, 0, unroll=True)
        pass_on(t - 1)
        return carry

    lax.fori_loop(1, PHASES, phase, 0)

    def last(piece, carry):
        for way in range(2):
            hop(PHASES - 1, way, piece).wait_recv()
            for t in range(PHASES - STAGES, PHASES):
                hop(t, way, piece).wait_send()
        return carry

    lax.fori_loop(0, PIECES, last, 0)
    pass_on(PHASES - 1)
    settle(PHASES - 2)
    settle(PHASES - 1)

    def drain(t, carry):
        for way in range(2):
            across(t, way, 1 - side).wait_recv()
        return carry

    lax.fori_loop(0, PHASES, drain, 0)
    for k in range(1, 16):
        vote(k, ring).wait_send()
        vote(k, lax.rem(ring + 16 - k, 16)).wait_recv()
    kept.wait()
    own_vote.wait()
    flag[...] = jnp.max(votes[...], axis=0)


def packets(source, pool, rest):
    dma = pltpu.SemaphoreType.DMA
    vmem = pl.BlockSpec(memory_space=pltpu.VMEM)
    return pl.pallas_call(
        packet_kernel,
        in_specs=[
            pl.BlockSpec(memory_space=pltpu.SMEM),
            vmem,
            vmem,
        ],
        out_specs=(pl.BlockSpec(memory_space=pl.ANY), vmem),
        out_shape=(
            jax.ShapeDtypeStruct((ENTRIES + UNITS,) + UNIT, jnp.bfloat16),
            jax.ShapeDtypeStruct((HEADS, 128), jnp.int32),
        ),
        scratch_shapes=[
            pltpu.VMEM((2, PHASES, SLOTS) + UNIT, jnp.bfloat16),
            pltpu.VMEM((2, STAGES, SLOTS) + UNIT, jnp.bfloat16),
            pltpu.VMEM((16, HEADS, 128), jnp.int32),
            dma((2, STAGES, PIECES)),
            dma((2, PHASES, PIECES)),
            dma((2, 2)),
            dma((2, 2)),
            dma((2, PHASES)),
            dma((2,)),
            dma((16,)),
            dma((16,)),
        ],
        compiler_params=pltpu.CompilerParams(
            collective_id=1, has_side_effects=True, vmem_limit_bytes=48 * 1024 * 1024
        ),
        name="packets",
    )(source, pool, rest)


def gather_kernel(
    fast, where, wanted, info, pool, query_pool, fetched, asked, held, held_asked, sems, out_sems
):
    first = info[HEADS]

    def spot(code, h):
        if fast:
            return where[h, code]
        return (code >> 3) * OWN + h * NB_DEV + (code & 7)

    def query_spot(g, h):
        unit = g * (QUNITS // G) + h // 2
        if not fast:
            return unit
        mine = first >> 3
        owner = info[HEADS + 1 + g] >> 3
        core = owner & 1
        delta = ((mine >> 1) - (owner >> 1)) & (CHIPS - 1)
        shared = (owner >> 1) == (info[HEADS + 1] >> 4)
        rank = jnp.where(shared, unit, h // 2)
        near = ENTRIES + core * QUNITS + unit
        step = jnp.where(delta <= 8, delta - 1, PHASES + CHIPS - delta - 1)
        far = (step * 2 + (rank & 1)) * SLOTS + (rank >> 1)
        return jnp.where(delta == 0, near, far)

    def copies(h):
        for i in range(FETCH):
            if i < NEAR:
                code = jnp.clip(first - WIN + i, 0, CODES - 1)
            elif i < NEAR + G:
                code = info[HEADS + 1 + i - NEAR]
            else:
                code = wanted[h * PICKS + i - NEAR - G]
            yield pltpu.make_async_copy(pool.at[spot(code, h)], held.at[h, i], sems.at[h, i])
        for g in range(G):
            yield pltpu.make_async_copy(
                query_pool.at[query_spot(g, h), h % 2], held_asked.at[h, g], sems.at[h, FETCH + g]
            )

    def start(h, carry):
        for copy in copies(h):
            copy.start()
        return carry

    def store(h):
        return (
            pltpu.make_async_copy(held.at[h], fetched.at[h], out_sems.at[h, 0]),
            pltpu.make_async_copy(held_asked.at[h], asked.at[h], out_sems.at[h, 1]),
        )

    def pass_on(h, carry):
        for i in range(FETCH):
            pltpu.make_async_copy(pool.at[0], held.at[h, i], sems.at[h, i]).wait()
        for g in range(G):
            pltpu.make_async_copy(
                query_pool.at[0, 0], held_asked.at[h, g], sems.at[h, FETCH + g]
            ).wait()
        for copy in store(h):
            copy.start()
        return carry

    def finish(h, carry):
        for copy in store(h):
            copy.wait()
        return carry

    lax.fori_loop(0, HEADS, start, 0)
    lax.fori_loop(0, HEADS, pass_on, 0)
    lax.fori_loop(0, HEADS, finish, 0)


def gather(fast, where, wanted, info, pool, query_pool):
    smem = pl.BlockSpec(memory_space=pltpu.SMEM)
    hbm = pl.BlockSpec(memory_space=pl.ANY)
    return pl.pallas_call(
        lambda *refs: gather_kernel(fast, *refs),
        in_specs=[smem, smem, smem, hbm, hbm],
        out_specs=(hbm, hbm),
        out_shape=(
            jax.ShapeDtypeStruct((HEADS, FETCH) + UNIT, jnp.bfloat16),
            jax.ShapeDtypeStruct((HEADS, G, BLOCK, WIDTH), jnp.bfloat16),
        ),
        scratch_shapes=[
            pltpu.VMEM((HEADS, FETCH) + UNIT, jnp.bfloat16),
            pltpu.VMEM((HEADS, G, BLOCK, WIDTH), jnp.bfloat16),
            pltpu.SemaphoreType.DMA((HEADS, FETCH + G)),
            pltpu.SemaphoreType.DMA((HEADS, 2)),
        ],
        compiler_params=pltpu.CompilerParams(vmem_limit_bytes=32 * 1024 * 1024),
        name="gather" if fast else "gather_slow",
    )(where, wanted, info, pool, query_pool)


HALF = HEADS // 2
SHARE = HALF * WIDTH // CHIPS


def attend_kernel(
    info, query, pairs, asked, fetched, out, merged,
    held, part, stats, theirs, their_stats, half, half_stats, got, got_stats, piece,
    load_sem, pair_send, pair_land, send, land, send_stats, land_stats, back, home,
):
    me = lax.axis_index("seq")
    chip, side = me // 2, lax.rem(me, 2)
    sibling = me + 1 - 2 * side
    peers = [lax.rem(chip + k, CHIPS) * 2 + side for k in range(1, CHIPS)]
    first = me * NB_DEV

    def load(h):
        return pltpu.make_async_copy(fetched.at[h], held.at[h], load_sem.at[h])

    for h in range(HEADS):
        load(h).start()
    greet([place(peer) for peer in peers] + [place(sibling)])

    def pair(i, source, target):
        return pltpu.make_async_remote_copy(
            src_ref=source,
            dst_ref=target,
            send_sem=pair_send.at[i],
            recv_sem=pair_land.at[i],
            device_id=place(sibling),
            device_id_type=MESH,
        )

    column = lax.broadcasted_iota(jnp.int32, (1, WKEYS), 1) // BLOCK - WIN
    contract = (((1,), (1,)), ((), ()))
    scale = 1.0 / math.sqrt(WIDTH)


    def one_partial(h, carry):
        own = pl.ds(h * NB_DEV, NB_DEV)
        scores = scale * lax.dot_general(
            pairs[own, 0].reshape(NB_DEV * BLOCK, WIDTH),
            asked[h].reshape(G * BLOCK, WIDTH),
            contract,
            preferred_element_type=jnp.float32,
        )
        peak = jnp.max(scores, axis=0, keepdims=True)
        weights = jnp.exp(scores - peak)
        sums = jnp.sum(weights, axis=0, keepdims=True)
        weighted = lax.dot_general(
            pairs[own, 1].reshape(NB_DEV * BLOCK, WIDTH),
            weights.astype(jnp.bfloat16),
            (((0,), (0,)), ((), ())),
            preferred_element_type=jnp.float32,
        )
        part[h] = (weighted / sums).astype(jnp.bfloat16)
        stats[h] = jnp.concatenate((peak, sums, jnp.zeros((6, WIDTH), jnp.float32)), axis=0)
        return carry

    def one_head(head, outer):
        load(head).wait()
        radius = info[head]

        def one_block(b, carry):
            rows = pl.ds(pl.multiple_of(b * BLOCK, BLOCK), BLOCK)
            q = query[head, rows]
            window = [b + i for i in range(2 * WIN + 1)]
            near_keys = jnp.concatenate([held[head, i, 0] for i in window], axis=0)
            near_values = jnp.concatenate([held[head, i, 1] for i in window], axis=0)
            others = [NEAR, NEAR + 1] + [NEAR + G + b * R + r for r in range(R)]
            far_keys = jnp.concatenate([held[head, i, 0] for i in others], axis=0)
            far_values = jnp.concatenate([held[head, i, 1] for i in others], axis=0)
            target = first + b + column
            usable = (jnp.abs(column) <= radius) & (target >= 0) & (target < CODES)
            near = lax.dot_general(q, near_keys, contract, preferred_element_type=jnp.float32)
            near = jnp.where(usable, near * scale, -jnp.inf)
            far = lax.dot_general(q, far_keys, contract, preferred_element_type=jnp.float32) * scale
            peak = jnp.maximum(
                jnp.max(near, axis=1, keepdims=True), jnp.max(far, axis=1, keepdims=True)
            )
            near = jnp.exp(near - peak)
            far = jnp.exp(far - peak)
            row_total = jnp.sum(near, axis=1, keepdims=True) + jnp.sum(far, axis=1, keepdims=True)
            weighted = jnp.dot(
                near.astype(jnp.bfloat16), near_values, preferred_element_type=jnp.float32
            ) + jnp.dot(far.astype(jnp.bfloat16), far_values, preferred_element_type=jnp.float32)
            out[head, rows] = (weighted / row_total).astype(jnp.bfloat16)
            return carry

        lax.fori_loop(0, NB_DEV, one_block, 0, unroll=2)
        return outer

    lax.fori_loop(0, HEADS, one_partial, 0)
    their_heads = pl.ds((1 - side) * HALF, HALF)
    my_heads = pl.ds(side * HALF, HALF)
    swaps = [
        pair(0, part.at[their_heads], theirs),
        pair(1, stats.at[their_heads], their_stats),
    ]
    for copy in swaps:
        copy.start()
    lax.fori_loop(0, 1, one_head, 0)
    for copy in swaps:
        copy.wait_recv()
    for h in range(HALF):
        mine = stats[side * HALF + h]
        other = their_stats[h]
        peak = jnp.maximum(mine[0:1, :], other[0:1, :])
        first = mine[1:2, :] * jnp.exp(mine[0:1, :] - peak)
        second = other[1:2, :] * jnp.exp(other[0:1, :] - peak)
        total = first + second
        weighted = (first / total) * part[side * HALF + h].astype(jnp.float32) + (
            second / total
        ) * theirs[h].astype(jnp.float32)
        half[h] = weighted.astype(jnp.bfloat16)
        half_stats[h : h + 1, :] = peak
        half_stats[HALF + h : HALF + h + 1, :] = total

    def rows(who):
        return who // 4, pl.ds(lax.rem(who, 4) * SHARE, SHARE)

    def hand(k, slot):
        to = lax.rem(chip + k, CHIPS)
        head, span = rows(to)
        weighted = pltpu.make_async_remote_copy(
            src_ref=half.at[head, span],
            dst_ref=got.at[slot],
            send_sem=send.at[k],
            recv_sem=land.at[k],
            device_id=place(to * 2 + side),
            device_id_type=MESH,
        )
        sums = pltpu.make_async_remote_copy(
            src_ref=half_stats,
            dst_ref=got_stats.at[slot],
            send_sem=send_stats.at[k],
            recv_sem=land_stats.at[k],
            device_id=place(to * 2 + side),
            device_id_type=MESH,
        )
        return weighted, sums

    def give(k, who):
        head, span = rows(who)
        return pltpu.make_async_remote_copy(
            src_ref=piece,
            dst_ref=merged.at[side * HALF + head, span],
            send_sem=back.at[k],
            recv_sem=home.at[k],
            device_id=place(lax.rem(chip + k, CHIPS) * 2 + side),
            device_id_type=MESH,
        )

    for k in range(1, CHIPS):
        for copy in hand(k, chip):
            copy.start()
    head, span = rows(chip)
    got[chip] = half[head, span]
    got_stats[chip] = half_stats[...]
    lax.fori_loop(1, 4, one_head, 0)
    for k in range(1, CHIPS):
        for copy in hand(k, lax.rem(chip + CHIPS - k, CHIPS)):
            copy.wait_recv()
    all_stats = got_stats[...]
    peaks = jnp.zeros((CHIPS, G * BLOCK), jnp.float32)
    sums = jnp.zeros((CHIPS, G * BLOCK), jnp.float32)
    for h in range(HALF):
        peaks = jnp.where(head == h, all_stats[:, h, :], peaks)
        sums = jnp.where(head == h, all_stats[:, HALF + h, :], sums)
    weights = sums * jnp.exp(peaks - jnp.max(peaks, axis=0, keepdims=True))
    weights = weights / jnp.sum(weights, axis=0, keepdims=True)
    total = jnp.zeros((SHARE, G * BLOCK), jnp.float32)
    for k in range(CHIPS):
        total = total + weights[k : k + 1, :] * got[k].astype(jnp.float32)
    piece[...] = total.astype(jnp.bfloat16)
    for k in range(1, CHIPS):
        give(k, chip).start()
    merged[side * HALF + head, span] = piece[...]
    lax.fori_loop(4, 7, one_head, 0)
    for k in range(1, CHIPS):
        give(k, lax.rem(chip + CHIPS - k, CHIPS)).wait_recv()
    last = pair(2, merged.at[my_heads], merged.at[my_heads])
    last.start()
    lax.fori_loop(7, HEADS, one_head, 0)
    for copy in swaps:
        copy.wait_send()
    for k in range(1, CHIPS):
        for copy in hand(k, chip):
            copy.wait_send()
        give(k, chip).wait_send()
    last.wait_send()
    pair(2, merged.at[their_heads], merged.at[their_heads]).wait_recv()


def attend(info, query, pairs, asked, fetched):
    dma = pltpu.SemaphoreType.DMA
    vmem = pl.BlockSpec(memory_space=pltpu.VMEM)
    rows = G * BLOCK
    return pl.pallas_call(
        attend_kernel,
        in_specs=[
            pl.BlockSpec(memory_space=pltpu.SMEM), vmem, vmem, vmem,
            pl.BlockSpec(memory_space=pl.ANY),
        ],
        out_specs=(vmem, vmem),
        out_shape=(
            jax.ShapeDtypeStruct((HEADS, NB_DEV * BLOCK, WIDTH), jnp.bfloat16),
            jax.ShapeDtypeStruct((HEADS, WIDTH, rows), jnp.bfloat16),
        ),
        scratch_shapes=[
            pltpu.VMEM((HEADS, FETCH) + UNIT, jnp.bfloat16),
            pltpu.VMEM((HEADS, WIDTH, rows), jnp.bfloat16),
            pltpu.VMEM((HEADS, 8, rows), jnp.float32),
            pltpu.VMEM((HALF, WIDTH, rows), jnp.bfloat16),
            pltpu.VMEM((HALF, 8, rows), jnp.float32),
            pltpu.VMEM((HALF, WIDTH, rows), jnp.bfloat16),
            pltpu.VMEM((2 * HALF, rows), jnp.float32),
            pltpu.VMEM((CHIPS, SHARE, rows), jnp.bfloat16),
            pltpu.VMEM((CHIPS, 2 * HALF, rows), jnp.float32),
            pltpu.VMEM((SHARE, rows), jnp.bfloat16),
            dma((HEADS,)),
        ]
        + [dma((3,))] * 2
        + [dma((CHIPS,))] * 6,
        compiler_params=pltpu.CompilerParams(
            collective_id=2, has_side_effects=True, vmem_limit_bytes=32 * 1024 * 1024
        ),
        name="attend",
    )(info, query, pairs, asked, fetched)


def local(queries, keys, values, window_radius, global_ids, rand_owner, rand_local):
    position = lax.axis_index("seq")
    block_ids = position * NB_DEV + jnp.arange(NB_DEV, dtype=jnp.int32)

    pairs = jnp.stack((keys, values)).reshape(2, NB_DEV, BLOCK, HEADS, WIDTH)
    pairs = pairs.transpose(3, 1, 0, 2, 4).reshape((OWN,) + UNIT)
    query_heads = queries.transpose(1, 0, 2)
    query_blocks = query_heads.reshape(HEADS, NB_DEV, BLOCK, WIDTH)
    units = jnp.concatenate(
        [
            lax.dynamic_index_in_dim(query_blocks, global_ids[g] % NB_DEV, axis=1, keepdims=False)
            for g in range(G)
        ]
    ).reshape((QUNITS,) + UNIT)
    wanted = (rand_owner[0] * NB_DEV + rand_local[0]).astype(jnp.int32)
    wanted = wanted.transpose(1, 0, 2).reshape(HEADS, PICKS)
    table, pool = exchange(jnp.pad(wanted, ((0, 0), (0, WIDTH - PICKS))), pairs, units)
    radius = jnp.broadcast_to(window_radius[:, None], (HEADS, CODES)).astype(jnp.int32)
    source, where, rest = plan(global_ids, table, radius)
    log, flag = packets(source, pool, rest)
    info = jnp.concatenate((window_radius, (position * NB_DEV)[None], global_ids)).astype(jnp.int32)
    asking = (where, wanted.reshape(-1), info)

    def from_packets(pairs, units, log):
        return gather(True, *asking, log, log)

    def from_gather(pairs, units, log):
        everything = lax.all_gather(pairs, "seq", axis=0, tiled=True)
        holder = jnp.repeat(global_ids // NB_DEV, QUNITS // G) == position
        asked = lax.psum(jnp.where(holder[:, None, None, None], units, 0), "seq")
        return gather(False, *asking, everything, asked)

    fetched, asked = lax.cond(jnp.max(flag) > 0, from_gather, from_packets, pairs, units, log)
    sparse, merged = attend(info, query_heads, pairs, asked, fetched)
    global_out = merged.reshape(HEADS, WIDTH, G, BLOCK).transpose(2, 3, 0, 1)

    result = sparse.reshape(HEADS, NB_DEV, BLOCK, WIDTH).transpose(1, 2, 0, 3)
    for slot in range(G):
        owned = global_ids[slot] == block_ids
        result = jnp.where(owned[:, None, None, None], global_out[slot][None], result)
    return result.reshape(NB_DEV * BLOCK, HEADS, WIDTH)


def solution(mesh):
    placed = (
        P(("dp", "seq"), "tensor", None),
        P(("dp", "seq"), "tensor", None),
        P(("dp", "seq"), "tensor", None),
        P(("dp", "tensor")),
        P("dp"),
        P("tensor", ("dp", "seq"), None, None),
        P("tensor", ("dp", "seq"), None, None),
    )
    return jax.shard_map(
        local,
        mesh=mesh,
        in_specs=placed,
        out_specs=P(("dp", "seq"), "tensor", None),
        check_vma=False,
    )
```

```python
import math

import jax
import jax.numpy as jnp
from jax import lax
from jax.experimental import pallas as pl
from jax.experimental.pallas import tpu as pltpu
from jax.sharding import PartitionSpec as P

BLOCK = 64
WIN = 3
G = 2
R = 3
NB_DEV = 8
HEADS = 8
WIDTH = 128
LISTED = 2 * WIN + 1 + G + R
PICKS = NB_DEV * R
NEAR = NB_DEV + 2 * WIN
FETCH = NEAR + G + PICKS

RUNS = 32
CHIPS = 16
CODES = RUNS * NB_DEV
OWN = HEADS * NB_DEV
QUNITS = 8
UNITS = 2 * QUNITS + 2 * OWN
SLOTS = 8
PHASES = 36
PIECES = 4
PIECE = SLOTS // PIECES
STAGES = 4
ENTRIES = 2 * PHASES * 2 * SLOTS
UNIT = (2, BLOCK, WIDTH)
MESH = pl.DeviceIdType.MESH


def place(seq):
    return (lax.axis_index("dp"), seq, lax.axis_index("tensor"))


def greet(devices):
    barrier = pltpu.get_barrier_semaphore()
    for device in devices:
        pl.semaphore_signal(barrier, inc=1, device_id=device, device_id_type=MESH)
    pl.semaphore_wait(barrier, len(devices))


def exchange_kernel(wanted, pairs, units, table, pool, send, land, kept_sem, pair_send, pair_land):
    me = lax.axis_index("seq")
    side = lax.rem(me, 2)
    greet([place(lax.rem(me + k, RUNS)) for k in range(1, RUNS)])
    parts = (
        (units, lambda who: pool.at[pl.ds(who * QUNITS, QUNITS)]),
        (pairs, lambda who: pool.at[pl.ds(2 * QUNITS + who * OWN, OWN)]),
    )

    def across(i, who):
        return pltpu.make_async_remote_copy(
            src_ref=parts[i][0],
            dst_ref=parts[i][1](who),
            send_sem=pair_send.at[i],
            recv_sem=pair_land.at[i],
            device_id=place(me + 1 - 2 * side),
            device_id_type=MESH,
        )

    def tell(k, slot):
        return pltpu.make_async_remote_copy(
            src_ref=wanted,
            dst_ref=table.at[slot],
            send_sem=send.at[k],
            recv_sem=land.at[k],
            device_id=place(lax.rem(me + k, RUNS)),
            device_id_type=MESH,
        )

    for k in range(1, RUNS):
        tell(k, me).start()
    kept = [pltpu.make_async_copy(wanted, table.at[me], kept_sem.at[2])]
    for i in range(2):
        across(i, side).start()
        kept.append(pltpu.make_async_copy(parts[i][0], parts[i][1](side), kept_sem.at[i]))
    for copy in kept:
        copy.start()
    for k in range(1, RUNS):
        tell(k, me).wait_send()
        tell(k, lax.rem(me + RUNS - k, RUNS)).wait_recv()
    for i in range(2):
        across(i, side).wait_send()
        across(i, 1 - side).wait_recv()
    for copy in kept:
        copy.wait()


def exchange(wanted, pairs, units):
    dma = pltpu.SemaphoreType.DMA
    vmem = pl.BlockSpec(memory_space=pltpu.VMEM)
    hbm = pl.BlockSpec(memory_space=pl.ANY)
    return pl.pallas_call(
        exchange_kernel,
        in_specs=[vmem, hbm, hbm],
        out_specs=(vmem, hbm),
        out_shape=(
            jax.ShapeDtypeStruct((RUNS, HEADS, WIDTH), jnp.int32),
            jax.ShapeDtypeStruct((UNITS,) + UNIT, jnp.bfloat16),
        ),
        scratch_shapes=[dma((RUNS,)), dma((RUNS,)), dma((3,)), dma((2,)), dma((2,))],
        compiler_params=pltpu.CompilerParams(collective_id=0, has_side_effects=True),
        name="exchange",
    )(wanted, pairs, units)


def plan_kernel(global_ids, table, radius, source, where, rest, keys, numbers, sems):
    me = lax.axis_index("seq")
    chip, side = me // 2, lax.rem(me, 2)
    shape = (HEADS, CODES)
    code = lax.broadcasted_iota(jnp.int32, shape, 1)
    row = lax.broadcasted_iota(jnp.int32, shape, 0)
    home = code >> 4
    first, second = global_ids[0], global_ids[1]
    everywhere = ((code == first) | (code == second)).astype(jnp.int32)

    def reaches(d, state):
        right, left, far = state
        picked = table[d]
        apart = code - d * NB_DEV
        beside = (apart >= -radius[...]) & (apart < NB_DEV + radius[...])
        hit = everywhere | beside.astype(jnp.int32)
        for k in range(PICKS):
            hit = hit | (picked[:, k : k + 1] == code).astype(jnp.int32)
        delta = ((d >> 1) - home) & (CHIPS - 1)
        right = jnp.maximum(right, jnp.where(delta < 8, hit * delta, 0))
        left = jnp.maximum(left, jnp.where(delta > 8, hit * (CHIPS - delta), 0))
        return right, left, far | jnp.where(delta == 8, hit, 0)

    zero = jnp.zeros(shape, jnp.int32)
    right, left, far = lax.fori_loop(0, RUNS, reaches, (zero, zero, zero))
    by_right = (right > left) | ((right == left) & (((row + code) & 1) == 0))
    right = jnp.where((far > 0) & by_right, 8, right)
    left = jnp.where((far > 0) & ~by_right, 8, left)

    lane_i = lax.broadcasted_iota(jnp.int32, (CODES, CODES), 0)
    lane_j = lax.broadcasted_iota(jnp.int32, (CODES, CODES), 1)
    together = (lane_i >> 4) == (lane_j >> 4)
    group = together.astype(jnp.bfloat16)
    before = (together & (lane_i < lane_j)).astype(jnp.bfloat16)
    holds_first = (home == (first >> 4)).astype(jnp.int32)
    holds_second = (home == (second >> 4)).astype(jnp.int32)
    asked = (holds_first + holds_second) * (QUNITS // G)

    def running_rows(x):
        height = x.shape[0]
        line = lax.broadcasted_iota(jnp.int32, x.shape, 0)
        step = 1
        while step < height:
            x = x + jnp.where(line >= step, pltpu.roll(x, step, 0), 0)
            step *= 2
        return x

    def last_row(x):
        return jnp.broadcast_to(x[x.shape[0] - 1 :, :], x.shape)

    def order(extent):
        rank = jnp.full(shape, 4096, jnp.int32)
        reach = [None] * 9
        above = asked
        for p in range(8, 0, -1):
            same = (extent == p).astype(jnp.bfloat16)
            in_group = jnp.dot(same, group, preferred_element_type=jnp.float32).astype(jnp.int32)
            ahead = jnp.dot(same, before, preferred_element_type=jnp.float32).astype(jnp.int32)
            running = running_rows(in_group)
            rank = jnp.where(extent == p, above + running - in_group + ahead, rank)
            above = above + last_row(running)
            reach[p] = above
        return rank, reach

    ways = [order(extent) for extent in (right, left)]
    wide = lambda x: jnp.concatenate((x, x), axis=0)
    reaches_wide = [[None] + [wide(x) for x in reach[1:]] for rank, reach in ways]

    def phase(t, state):
        after = []
        for way in range(2):
            rank, reach = ways[way][0], reaches_wide[way]
            going, queue, key = state[3 * way : 3 * way + 3]
            free = (going == 0).astype(jnp.int32)
            running = running_rows(free)
            nth = running - free
            number = queue + nth
            fresh = (free > 0) & (number < reach[1])
            extent = sum((number < reach[p]).astype(jnp.int32) for p in range(1, 9))
            going = jnp.where(fresh, extent, going)
            taken = jnp.minimum(queue + last_row(running), reach[1])
            mark = jnp.where(fresh, number, -1)
            for s in range(2 * SLOTS):
                here = rank == jnp.broadcast_to(mark[s : s + 1, :], shape)
                key = jnp.where(here, t * 2 * SLOTS + s, key)
            going = jnp.maximum(pltpu.roll(going, 16 if way == 0 else CODES - 16, 1) - 1, 0)
            after += [going, taken, key]
        return tuple(after)

    state = lax.fori_loop(0, PHASES, phase, (wide(zero), wide(zero), zero) * 2)
    over = wide(zero)
    for way in range(2):
        over = over + state[3 * way] + reaches_wide[way][1] - state[3 * way + 1]
    over = over[:HEADS] + over[HEADS:]
    rest[...] = over[:, :128] + over[:, 128:]

    delta = (chip - home) & (CHIPS - 1)
    core = (code >> 3) & 1
    near = ENTRIES + 2 * QUNITS + core * OWN + row * NB_DEV + (code & 7)
    goes = [(state[2] >> 4) + delta - 1, PHASES + (state[5] >> 4) + CHIPS - delta - 1]
    slots = [state[2] & 15, state[5] & 15]
    entry = [(goes[way] * 2 + (slots[way] & 1)) * SLOTS + (slots[way] >> 1) for way in range(2)]
    from_left = (delta < 8) | ((delta == 8) & (right == 8))
    far_entry = jnp.clip(jnp.where(from_left, entry[0], entry[1]), 0, ENTRIES - 1)
    where[...] = jnp.where(delta == 0, near, far_entry)

    for way in range(2):
        rank, reach = ways[way]
        sent = rank < state[3 * way + 1][:HEADS]
        keys[way] = jnp.where(sent, state[3 * way + 2], -1)
    fetch = pltpu.make_async_copy(keys, numbers, sems)
    fetch.start()
    fetch.wait()

    def clear(i, carry):
        source[i] = -1
        return carry

    lax.fori_loop(0, 2 * PHASES * SLOTS, clear, 0, unroll=8)
    base = chip * 2 * NB_DEV
    has = [chip == (first >> 4), chip == (second >> 4)]
    count = (has[0].astype(jnp.int32) + has[1].astype(jnp.int32)) * (QUNITS // G)
    for way in range(2):

        def put(i, carry):
            lane = i & 15
            key = numbers[way, i >> 4, base + lane]

            @pl.when((key >= 0) & ((key & 1) == side))
            def _():
                unit = 2 * QUNITS + (lane >> 3) * OWN + (i >> 4) * NB_DEV + (lane & 7)
                source[way * PHASES * SLOTS + (key >> 1)] = unit

            return carry

        lax.fori_loop(0, 2 * OWN, put, 0, unroll=4)
        for r in range(QUNITS):
            late = jnp.logical_not(has[0]) if r < QUNITS // G else True
            late = jnp.asarray(late)
            core = (jnp.where(late, second, first) >> 3) & 1
            unit = core * QUNITS + jnp.where(late, QUNITS // G, 0) + r % (QUNITS // G)

            @pl.when((r < count) & (side == r % 2))
            def _():
                source[way * PHASES * SLOTS + r // 2] = unit


def plan(global_ids, table, radius):
    vmem = pl.BlockSpec(memory_space=pltpu.VMEM)
    smem = pl.BlockSpec(memory_space=pltpu.SMEM)
    return pl.pallas_call(
        plan_kernel,
        in_specs=[smem, vmem, vmem],
        out_specs=(smem, vmem, vmem),
        out_shape=(
            jax.ShapeDtypeStruct((2 * PHASES * SLOTS,), jnp.int32),
            jax.ShapeDtypeStruct((HEADS, CODES), jnp.int32),
            jax.ShapeDtypeStruct((HEADS, 128), jnp.int32),
        ),
        scratch_shapes=[
            pltpu.VMEM((2, HEADS, CODES), jnp.int32),
            pltpu.SMEM((2, HEADS, CODES), jnp.int32),
            pltpu.SemaphoreType.DMA(()),
        ],
        name="plan",
    )(global_ids, table, radius)


def packet_kernel(
    source, pool, rest, log, flag, recv, stage, votes,
    send_sem, land_sem, keep_sem, across_sem, across_land, tail_sem, vote_send, vote_land,
):
    me = lax.axis_index("seq")
    chip, side = me // 2, lax.rem(me, 2)
    sibling = me + 1 - 2 * side
    ahead = lax.rem(chip + 1, CHIPS) * 2 + side
    behind = lax.rem(chip + CHIPS - 1, CHIPS) * 2 + side
    dp, tensor = lax.axis_index("dp"), lax.axis_index("tensor")
    ring = dp * 8 + tensor

    def other(k):
        there = lax.rem(ring + k, 16)
        return (there // 8, me, lax.rem(there, 8))

    greet([place(ahead), place(behind), place(sibling)] + [other(k) for k in range(1, 16)])

    def vote(k, slot):
        return pltpu.make_async_remote_copy(
            src_ref=rest,
            dst_ref=votes.at[slot],
            send_sem=vote_send.at[k],
            recv_sem=vote_land.at[k],
            device_id=other(k),
            device_id_type=MESH,
        )

    for k in range(1, 16):
        vote(k, ring).start()
    kept = pltpu.make_async_copy(pool, log.at[pl.ds(ENTRIES, UNITS)], tail_sem.at[0])
    kept.start()
    own_vote = pltpu.make_async_copy(rest, votes.at[ring], tail_sem.at[1])
    own_vote.start()

    def hop(t, way, piece):
        rows = pl.ds(piece * PIECE, PIECE)
        return pltpu.make_async_remote_copy(
            src_ref=stage.at[way, lax.rem(t, STAGES), rows],
            dst_ref=recv.at[way, t, rows],
            send_sem=send_sem.at[way, lax.rem(t, STAGES), piece],
            recv_sem=land_sem.at[way, t, piece],
            device_id=place(ahead if way == 0 else behind),
            device_id_type=MESH,
        )

    def entry(t, way, who):
        return pl.ds(((way * PHASES + t) * 2 + who) * SLOTS, SLOTS)

    def keep(t, way):
        return pltpu.make_async_copy(
            recv.at[way, t], log.at[entry(t, way, side)], keep_sem.at[way, lax.rem(t, 2)]
        )

    def across(t, way, who):
        return pltpu.make_async_remote_copy(
            src_ref=recv.at[way, t],
            dst_ref=log.at[entry(t, way, who)],
            send_sem=across_sem.at[way, lax.rem(t, 2)],
            recv_sem=across_land.at[way, t],
            device_id=place(sibling),
            device_id_type=MESH,
        )

    def compose(t, way, piece, first):
        for i in range(PIECE):
            slot = piece * PIECE + i
            wanted = source[(way * PHASES + t) * SLOTS + slot]
            unit = pool[jnp.maximum(wanted, 0)]
            if not first:
                unit = jnp.where(wanted >= 0, unit, recv[way, t - 1, slot])
            stage[way, lax.rem(t, STAGES), slot] = unit

    for piece in range(PIECES):
        for way in range(2):
            compose(0, way, piece, True)
            hop(0, way, piece).start()

    def settle(t):
        for way in range(2):
            keep(t, way).wait()
            across(t, way, side).wait_send()

    def pass_on(t):
        pl.when(t >= 2)(lambda: settle(t - 2))
        for way in range(2):
            keep(t, way).start()
            across(t, way, side).start()

    def phase(t, carry):
        def step(piece, inner):
            for way in range(2):
                hop(t - 1, way, piece).wait_recv()
                pl.when(t >= STAGES)(lambda: hop(t - STAGES, way, piece).wait_send())
                compose(t, way, piece, False)
                hop(t, way, piece).start()
            return inner

        lax.fori_loop(0, PIECES, step, 0, unroll=True)
        pass_on(t - 1)
        return carry

    lax.fori_loop(1, PHASES, phase, 0)

    def last(piece, carry):
        for way in range(2):
            hop(PHASES - 1, way, piece).wait_recv()
            for t in range(PHASES - STAGES, PHASES):
                hop(t, way, piece).wait_send()
        return carry

    lax.fori_loop(0, PIECES, last, 0)
    pass_on(PHASES - 1)
    settle(PHASES - 2)
    settle(PHASES - 1)

    def drain(t, carry):
        for way in range(2):
            across(t, way, 1 - side).wait_recv()
        return carry

    lax.fori_loop(0, PHASES, drain, 0)
    for k in range(1, 16):
        vote(k, ring).wait_send()
        vote(k, lax.rem(ring + 16 - k, 16)).wait_recv()
    kept.wait()
    own_vote.wait()
    flag[...] = jnp.max(votes[...], axis=0)


def packets(source, pool, rest):
    dma = pltpu.SemaphoreType.DMA
    vmem = pl.BlockSpec(memory_space=pltpu.VMEM)
    return pl.pallas_call(
        packet_kernel,
        in_specs=[
            pl.BlockSpec(memory_space=pltpu.SMEM),
            vmem,
            vmem,
        ],
        out_specs=(pl.BlockSpec(memory_space=pl.ANY), vmem),
        out_shape=(
            jax.ShapeDtypeStruct((ENTRIES + UNITS,) + UNIT, jnp.bfloat16),
            jax.ShapeDtypeStruct((HEADS, 128), jnp.int32),
        ),
        scratch_shapes=[
            pltpu.VMEM((2, PHASES, SLOTS) + UNIT, jnp.bfloat16),
            pltpu.VMEM((2, STAGES, SLOTS) + UNIT, jnp.bfloat16),
            pltpu.VMEM((16, HEADS, 128), jnp.int32),
            dma((2, STAGES, PIECES)),
            dma((2, PHASES, PIECES)),
            dma((2, 2)),
            dma((2, 2)),
            dma((2, PHASES)),
            dma((2,)),
            dma((16,)),
            dma((16,)),
        ],
        compiler_params=pltpu.CompilerParams(
            collective_id=1, has_side_effects=True, vmem_limit_bytes=48 * 1024 * 1024
        ),
        name="packets",
    )(source, pool, rest)


def gather_kernel(
    fast, where, wanted, info, pool, query_pool, fetched, asked, held, held_asked, sems, out_sems
):
    first = info[HEADS]

    def spot(code, h):
        if fast:
            return where[h, code]
        return (code >> 3) * OWN + h * NB_DEV + (code & 7)

    def query_spot(g, h):
        unit = g * (QUNITS // G) + h // 2
        if not fast:
            return unit
        mine = first >> 3
        owner = info[HEADS + 1 + g] >> 3
        core = owner & 1
        delta = ((mine >> 1) - (owner >> 1)) & (CHIPS - 1)
        shared = (owner >> 1) == (info[HEADS + 1] >> 4)
        rank = jnp.where(shared, unit, h // 2)
        near = ENTRIES + core * QUNITS + unit
        step = jnp.where(delta <= 8, delta - 1, PHASES + CHIPS - delta - 1)
        far = (step * 2 + (rank & 1)) * SLOTS + (rank >> 1)
        return jnp.where(delta == 0, near, far)

    def copies(h):
        for i in range(FETCH):
            if i < NEAR:
                code = jnp.clip(first - WIN + i, 0, CODES - 1)
            elif i < NEAR + G:
                code = info[HEADS + 1 + i - NEAR]
            else:
                code = wanted[h * PICKS + i - NEAR - G]
            yield pltpu.make_async_copy(pool.at[spot(code, h)], held.at[h, i], sems.at[h, i])
        for g in range(G):
            yield pltpu.make_async_copy(
                query_pool.at[query_spot(g, h), h % 2], held_asked.at[h, g], sems.at[h, FETCH + g]
            )

    def start(h, carry):
        for copy in copies(h):
            copy.start()
        return carry

    def store(h):
        return (
            pltpu.make_async_copy(held.at[h], fetched.at[h], out_sems.at[h, 0]),
            pltpu.make_async_copy(held_asked.at[h], asked.at[h], out_sems.at[h, 1]),
        )

    def pass_on(h, carry):
        for i in range(FETCH):
            pltpu.make_async_copy(pool.at[0], held.at[h, i], sems.at[h, i]).wait()
        for g in range(G):
            pltpu.make_async_copy(
                query_pool.at[0, 0], held_asked.at[h, g], sems.at[h, FETCH + g]
            ).wait()
        for copy in store(h):
            copy.start()
        return carry

    def finish(h, carry):
        for copy in store(h):
            copy.wait()
        return carry

    lax.fori_loop(0, HEADS, start, 0)
    lax.fori_loop(0, HEADS, pass_on, 0)
    lax.fori_loop(0, HEADS, finish, 0)


def gather(fast, where, wanted, info, pool, query_pool):
    smem = pl.BlockSpec(memory_space=pltpu.SMEM)
    hbm = pl.BlockSpec(memory_space=pl.ANY)
    return pl.pallas_call(
        lambda *refs: gather_kernel(fast, *refs),
        in_specs=[smem, smem, smem, hbm, hbm],
        out_specs=(hbm, hbm),
        out_shape=(
            jax.ShapeDtypeStruct((HEADS, FETCH) + UNIT, jnp.bfloat16),
            jax.ShapeDtypeStruct((HEADS, G, BLOCK, WIDTH), jnp.bfloat16),
        ),
        scratch_shapes=[
            pltpu.VMEM((HEADS, FETCH) + UNIT, jnp.bfloat16),
            pltpu.VMEM((HEADS, G, BLOCK, WIDTH), jnp.bfloat16),
            pltpu.SemaphoreType.DMA((HEADS, FETCH + G)),
            pltpu.SemaphoreType.DMA((HEADS, 2)),
        ],
        compiler_params=pltpu.CompilerParams(vmem_limit_bytes=32 * 1024 * 1024),
        name="gather" if fast else "gather_slow",
    )(where, wanted, info, pool, query_pool)


HALF = HEADS // 2
SHARE = HALF * WIDTH // CHIPS


def attend_kernel(
    info, query, pairs, asked, fetched, out, merged,
    held, part, stats, theirs, their_stats, half, half_stats, got, got_stats, piece,
    load_sem, pair_send, pair_land, send, land, send_stats, land_stats, back, home,
):
    me = lax.axis_index("seq")
    chip, side = me // 2, lax.rem(me, 2)
    sibling = me + 1 - 2 * side
    peers = [lax.rem(chip + k, CHIPS) * 2 + side for k in range(1, CHIPS)]
    first = me * NB_DEV

    def load(h):
        return pltpu.make_async_copy(fetched.at[h], held.at[h], load_sem.at[h])

    for h in range(HEADS):
        load(h).start()
    greet([place(peer) for peer in peers] + [place(sibling)])

    def pair(i, source, target):
        return pltpu.make_async_remote_copy(
            src_ref=source,
            dst_ref=target,
            send_sem=pair_send.at[i],
            recv_sem=pair_land.at[i],
            device_id=place(sibling),
            device_id_type=MESH,
        )

    column = lax.broadcasted_iota(jnp.int32, (1, LISTED * BLOCK), 1) // BLOCK - WIN
    contract = (((1,), (1,)), ((), ()))
    scale = 1.0 / math.sqrt(WIDTH)


    def one_partial(h, carry):
        own = pl.ds(h * NB_DEV, NB_DEV)
        scores = scale * lax.dot_general(
            pairs[own, 0].reshape(NB_DEV * BLOCK, WIDTH),
            asked[h].reshape(G * BLOCK, WIDTH),
            contract,
            preferred_element_type=jnp.float32,
        )
        peak = jnp.max(scores, axis=0, keepdims=True)
        weights = jnp.exp(scores - peak)
        sums = jnp.sum(weights, axis=0, keepdims=True)
        weighted = lax.dot_general(
            pairs[own, 1].reshape(NB_DEV * BLOCK, WIDTH),
            weights.astype(jnp.bfloat16),
            (((0,), (0,)), ((), ())),
            preferred_element_type=jnp.float32,
        )
        part[h] = (weighted / sums).astype(jnp.bfloat16)
        stats[h] = jnp.concatenate((peak, sums, jnp.zeros((6, WIDTH), jnp.float32)), axis=0)
        return carry

    def one_head(head, outer):
        load(head).wait()
        radius = info[head]

        def one_block(b, carry):
            rows = pl.ds(pl.multiple_of(b * BLOCK, BLOCK), BLOCK)
            units = [b + i for i in range(2 * WIN + 1)] + [NEAR, NEAR + 1]
            units = units + [NEAR + G + b * R + r for r in range(R)]
            held_keys = jnp.concatenate([held[head, i, 0] for i in units], axis=0)
            held_values = jnp.concatenate([held[head, i, 1] for i in units], axis=0)
            target = first + b + column
            inside = (jnp.abs(column) <= radius) & (target >= 0) & (target < CODES)
            usable = inside | (column > WIN)
            scores = scale * lax.dot_general(
                query[head, rows], held_keys, contract, preferred_element_type=jnp.float32
            )
            scores = jnp.where(usable, scores, -jnp.inf)
            weights = jnp.exp(scores - jnp.max(scores, axis=1, keepdims=True))
            row_total = jnp.sum(weights, axis=1, keepdims=True)
            weighted = jnp.dot(
                weights.astype(jnp.bfloat16), held_values, preferred_element_type=jnp.float32
            )
            out[head, rows] = (weighted / row_total).astype(jnp.bfloat16)
            return carry

        lax.fori_loop(0, NB_DEV, one_block, 0, unroll=4)
        return outer

    lax.fori_loop(0, HEADS, one_partial, 0)
    their_heads = pl.ds((1 - side) * HALF, HALF)
    my_heads = pl.ds(side * HALF, HALF)
    swaps = [
        pair(0, part.at[their_heads], theirs),
        pair(1, stats.at[their_heads], their_stats),
    ]
    for copy in swaps:
        copy.start()
    lax.fori_loop(0, 1, one_head, 0)
    for copy in swaps:
        copy.wait_recv()
    for h in range(HALF):
        mine = stats[side * HALF + h]
        other = their_stats[h]
        peak = jnp.maximum(mine[0:1, :], other[0:1, :])
        first = mine[1:2, :] * jnp.exp(mine[0:1, :] - peak)
        second = other[1:2, :] * jnp.exp(other[0:1, :] - peak)
        total = first + second
        weighted = (first / total) * part[side * HALF + h].astype(jnp.float32) + (
            second / total
        ) * theirs[h].astype(jnp.float32)
        half[h] = weighted.astype(jnp.bfloat16)
        half_stats[h : h + 1, :] = peak
        half_stats[HALF + h : HALF + h + 1, :] = total

    def rows(who):
        return who // 4, pl.ds(lax.rem(who, 4) * SHARE, SHARE)

    def hand(k, slot):
        to = lax.rem(chip + k, CHIPS)
        head, span = rows(to)
        weighted = pltpu.make_async_remote_copy(
            src_ref=half.at[head, span],
            dst_ref=got.at[slot],
            send_sem=send.at[k],
            recv_sem=land.at[k],
            device_id=place(to * 2 + side),
            device_id_type=MESH,
        )
        sums = pltpu.make_async_remote_copy(
            src_ref=half_stats,
            dst_ref=got_stats.at[slot],
            send_sem=send_stats.at[k],
            recv_sem=land_stats.at[k],
            device_id=place(to * 2 + side),
            device_id_type=MESH,
        )
        return weighted, sums

    def give(k, who):
        head, span = rows(who)
        return pltpu.make_async_remote_copy(
            src_ref=piece,
            dst_ref=merged.at[side * HALF + head, span],
            send_sem=back.at[k],
            recv_sem=home.at[k],
            device_id=place(lax.rem(chip + k, CHIPS) * 2 + side),
            device_id_type=MESH,
        )

    for k in range(1, CHIPS):
        for copy in hand(k, chip):
            copy.start()
    head, span = rows(chip)
    got[chip] = half[head, span]
    got_stats[chip] = half_stats[...]
    lax.fori_loop(1, 4, one_head, 0)
    for k in range(1, CHIPS):
        for copy in hand(k, lax.rem(chip + CHIPS - k, CHIPS)):
            copy.wait_recv()
    all_stats = got_stats[...]
    peaks = jnp.zeros((CHIPS, G * BLOCK), jnp.float32)
    sums = jnp.zeros((CHIPS, G * BLOCK), jnp.float32)
    for h in range(HALF):
        peaks = jnp.where(head == h, all_stats[:, h, :], peaks)
        sums = jnp.where(head == h, all_stats[:, HALF + h, :], sums)
    weights = sums * jnp.exp(peaks - jnp.max(peaks, axis=0, keepdims=True))
    weights = weights / jnp.sum(weights, axis=0, keepdims=True)
    total = jnp.zeros((SHARE, G * BLOCK), jnp.float32)
    for k in range(CHIPS):
        total = total + weights[k : k + 1, :] * got[k].astype(jnp.float32)
    piece[...] = total.astype(jnp.bfloat16)
    for k in range(1, CHIPS):
        give(k, chip).start()
    merged[side * HALF + head, span] = piece[...]
    lax.fori_loop(4, 7, one_head, 0)
    for k in range(1, CHIPS):
        give(k, lax.rem(chip + CHIPS - k, CHIPS)).wait_recv()
    last = pair(2, merged.at[my_heads], merged.at[my_heads])
    last.start()
    lax.fori_loop(7, HEADS, one_head, 0)
    for copy in swaps:
        copy.wait_send()
    for k in range(1, CHIPS):
        for copy in hand(k, chip):
            copy.wait_send()
        give(k, chip).wait_send()
    last.wait_send()
    pair(2, merged.at[their_heads], merged.at[their_heads]).wait_recv()


def attend(info, query, pairs, asked, fetched):
    dma = pltpu.SemaphoreType.DMA
    vmem = pl.BlockSpec(memory_space=pltpu.VMEM)
    rows = G * BLOCK
    return pl.pallas_call(
        attend_kernel,
        in_specs=[
            pl.BlockSpec(memory_space=pltpu.SMEM), vmem, vmem, vmem,
            pl.BlockSpec(memory_space=pl.ANY),
        ],
        out_specs=(vmem, vmem),
        out_shape=(
            jax.ShapeDtypeStruct((HEADS, NB_DEV * BLOCK, WIDTH), jnp.bfloat16),
            jax.ShapeDtypeStruct((HEADS, WIDTH, rows), jnp.bfloat16),
        ),
        scratch_shapes=[
            pltpu.VMEM((HEADS, FETCH) + UNIT, jnp.bfloat16),
            pltpu.VMEM((HEADS, WIDTH, rows), jnp.bfloat16),
            pltpu.VMEM((HEADS, 8, rows), jnp.float32),
            pltpu.VMEM((HALF, WIDTH, rows), jnp.bfloat16),
            pltpu.VMEM((HALF, 8, rows), jnp.float32),
            pltpu.VMEM((HALF, WIDTH, rows), jnp.bfloat16),
            pltpu.VMEM((2 * HALF, rows), jnp.float32),
            pltpu.VMEM((CHIPS, SHARE, rows), jnp.bfloat16),
            pltpu.VMEM((CHIPS, 2 * HALF, rows), jnp.float32),
            pltpu.VMEM((SHARE, rows), jnp.bfloat16),
            dma((HEADS,)),
        ]
        + [dma((3,))] * 2
        + [dma((CHIPS,))] * 6,
        compiler_params=pltpu.CompilerParams(
            collective_id=2, has_side_effects=True, vmem_limit_bytes=32 * 1024 * 1024
        ),
        name="attend",
    )(info, query, pairs, asked, fetched)


def local(queries, keys, values, window_radius, global_ids, rand_owner, rand_local):
    position = lax.axis_index("seq")
    block_ids = position * NB_DEV + jnp.arange(NB_DEV, dtype=jnp.int32)

    pairs = jnp.stack((keys, values)).reshape(2, NB_DEV, BLOCK, HEADS, WIDTH)
    pairs = pairs.transpose(3, 1, 0, 2, 4).reshape((OWN,) + UNIT)
    query_heads = queries.transpose(1, 0, 2)
    query_blocks = query_heads.reshape(HEADS, NB_DEV, BLOCK, WIDTH)
    units = jnp.concatenate(
        [
            lax.dynamic_index_in_dim(query_blocks, global_ids[g] % NB_DEV, axis=1, keepdims=False)
            for g in range(G)
        ]
    ).reshape((QUNITS,) + UNIT)
    wanted = (rand_owner[0] * NB_DEV + rand_local[0]).astype(jnp.int32)
    wanted = wanted.transpose(1, 0, 2).reshape(HEADS, PICKS)
    table, pool = exchange(jnp.pad(wanted, ((0, 0), (0, WIDTH - PICKS))), pairs, units)
    radius = jnp.broadcast_to(window_radius[:, None], (HEADS, CODES)).astype(jnp.int32)
    source, where, rest = plan(global_ids, table, radius)
    log, flag = packets(source, pool, rest)
    info = jnp.concatenate((window_radius, (position * NB_DEV)[None], global_ids)).astype(jnp.int32)
    asking = (where, wanted.reshape(-1), info)

    def from_packets(pairs, units, log):
        return gather(True, *asking, log, log)

    def from_gather(pairs, units, log):
        everything = lax.all_gather(pairs, "seq", axis=0, tiled=True)
        holder = jnp.repeat(global_ids // NB_DEV, QUNITS // G) == position
        asked = lax.psum(jnp.where(holder[:, None, None, None], units, 0), "seq")
        return gather(False, *asking, everything, asked)

    fetched, asked = lax.cond(jnp.max(flag) > 0, from_gather, from_packets, pairs, units, log)
    sparse, merged = attend(info, query_heads, pairs, asked, fetched)
    global_out = merged.reshape(HEADS, WIDTH, G, BLOCK).transpose(2, 3, 0, 1)

    result = sparse.reshape(HEADS, NB_DEV, BLOCK, WIDTH).transpose(1, 2, 0, 3)
    for slot in range(G):
        owned = global_ids[slot] == block_ids
        result = jnp.where(owned[:, None, None, None], global_out[slot][None], result)
    return result.reshape(NB_DEV * BLOCK, HEADS, WIDTH)


def solution(mesh):
    placed = (
        P(("dp", "seq"), "tensor", None),
        P(("dp", "seq"), "tensor", None),
        P(("dp", "seq"), "tensor", None),
        P(("dp", "tensor")),
        P("dp"),
        P("tensor", ("dp", "seq"), None, None),
        P("tensor", ("dp", "seq"), None, None),
    )
    return jax.shard_map(
        local,
        mesh=mesh,
        in_specs=placed,
        out_specs=P(("dp", "seq"), "tensor", None),
        check_vma=False,
    )
```

```python
import math

import jax
import jax.numpy as jnp
from jax import lax
from jax.experimental import pallas as pl
from jax.experimental.pallas import tpu as pltpu
from jax.sharding import PartitionSpec as P

BLOCK = 64
WIN = 3
G = 2
R = 3
NB_DEV = 8
HEADS = 8
WIDTH = 128
LISTED = 2 * WIN + 1 + G + R
PICKS = NB_DEV * R
NEAR = NB_DEV + 2 * WIN
FETCH = NEAR + G + PICKS

RUNS = 32
CHIPS = 16
CODES = RUNS * NB_DEV
OWN = HEADS * NB_DEV
QUNITS = 8
UNITS = 2 * QUNITS + 2 * OWN
SLOTS = 8
PHASES = 36
PIECES = 4
PIECE = SLOTS // PIECES
STAGES = 4
ENTRIES = 2 * PHASES * 2 * SLOTS
UNIT = (2, BLOCK, WIDTH)
MESH = pl.DeviceIdType.MESH


def place(seq):
    return (lax.axis_index("dp"), seq, lax.axis_index("tensor"))


def greet(devices):
    barrier = pltpu.get_barrier_semaphore()
    for device in devices:
        pl.semaphore_signal(barrier, inc=1, device_id=device, device_id_type=MESH)
    pl.semaphore_wait(barrier, len(devices))


def exchange_kernel(wanted, pairs, units, table, pool, send, land, kept_sem, pair_send, pair_land):
    me = lax.axis_index("seq")
    side = lax.rem(me, 2)
    greet([place(lax.rem(me + k, RUNS)) for k in range(1, RUNS)])
    parts = (
        (units, lambda who: pool.at[pl.ds(who * QUNITS, QUNITS)]),
        (pairs, lambda who: pool.at[pl.ds(2 * QUNITS + who * OWN, OWN)]),
    )

    def across(i, who):
        return pltpu.make_async_remote_copy(
            src_ref=parts[i][0],
            dst_ref=parts[i][1](who),
            send_sem=pair_send.at[i],
            recv_sem=pair_land.at[i],
            device_id=place(me + 1 - 2 * side),
            device_id_type=MESH,
        )

    def tell(k, slot):
        return pltpu.make_async_remote_copy(
            src_ref=wanted,
            dst_ref=table.at[slot],
            send_sem=send.at[k],
            recv_sem=land.at[k],
            device_id=place(lax.rem(me + k, RUNS)),
            device_id_type=MESH,
        )

    for k in range(1, RUNS):
        tell(k, me).start()
    kept = [pltpu.make_async_copy(wanted, table.at[me], kept_sem.at[2])]
    for i in range(2):
        across(i, side).start()
        kept.append(pltpu.make_async_copy(parts[i][0], parts[i][1](side), kept_sem.at[i]))
    for copy in kept:
        copy.start()
    for k in range(1, RUNS):
        tell(k, me).wait_send()
        tell(k, lax.rem(me + RUNS - k, RUNS)).wait_recv()
    for i in range(2):
        across(i, side).wait_send()
        across(i, 1 - side).wait_recv()
    for copy in kept:
        copy.wait()


def exchange(wanted, pairs, units):
    dma = pltpu.SemaphoreType.DMA
    vmem = pl.BlockSpec(memory_space=pltpu.VMEM)
    hbm = pl.BlockSpec(memory_space=pl.ANY)
    return pl.pallas_call(
        exchange_kernel,
        in_specs=[vmem, hbm, hbm],
        out_specs=(vmem, hbm),
        out_shape=(
            jax.ShapeDtypeStruct((RUNS, HEADS, WIDTH), jnp.int32),
            jax.ShapeDtypeStruct((UNITS,) + UNIT, jnp.bfloat16),
        ),
        scratch_shapes=[dma((RUNS,)), dma((RUNS,)), dma((3,)), dma((2,)), dma((2,))],
        compiler_params=pltpu.CompilerParams(collective_id=0, has_side_effects=True),
        name="exchange",
    )(wanted, pairs, units)


def plan_kernel(global_ids, table, radius, source, where, rest, keys, numbers, sems):
    me = lax.axis_index("seq")
    chip, side = me // 2, lax.rem(me, 2)
    shape = (HEADS, CODES)
    code = lax.broadcasted_iota(jnp.int32, shape, 1)
    row = lax.broadcasted_iota(jnp.int32, shape, 0)
    home = code >> 4
    first, second = global_ids[0], global_ids[1]
    everywhere = ((code == first) | (code == second)).astype(jnp.int32)

    def reaches(d, state):
        right, left, far = state
        picked = table[d]
        apart = code - d * NB_DEV
        beside = (apart >= -radius[...]) & (apart < NB_DEV + radius[...])
        hit = everywhere | beside.astype(jnp.int32)
        for k in range(PICKS):
            hit = hit | (picked[:, k : k + 1] == code).astype(jnp.int32)
        delta = ((d >> 1) - home) & (CHIPS - 1)
        right = jnp.maximum(right, jnp.where(delta < 8, hit * delta, 0))
        left = jnp.maximum(left, jnp.where(delta > 8, hit * (CHIPS - delta), 0))
        return right, left, far | jnp.where(delta == 8, hit, 0)

    zero = jnp.zeros(shape, jnp.int32)
    right, left, far = lax.fori_loop(0, RUNS, reaches, (zero, zero, zero))
    by_right = (right > left) | ((right == left) & (((row + code) & 1) == 0))
    right = jnp.where((far > 0) & by_right, 8, right)
    left = jnp.where((far > 0) & ~by_right, 8, left)

    lane_i = lax.broadcasted_iota(jnp.int32, (CODES, CODES), 0)
    lane_j = lax.broadcasted_iota(jnp.int32, (CODES, CODES), 1)
    together = (lane_i >> 4) == (lane_j >> 4)
    group = together.astype(jnp.bfloat16)
    before = (together & (lane_i < lane_j)).astype(jnp.bfloat16)
    holds_first = (home == (first >> 4)).astype(jnp.int32)
    holds_second = (home == (second >> 4)).astype(jnp.int32)
    asked = (holds_first + holds_second) * (QUNITS // G)

    def running_rows(x):
        height = x.shape[0]
        line = lax.broadcasted_iota(jnp.int32, x.shape, 0)
        step = 1
        while step < height:
            x = x + jnp.where(line >= step, pltpu.roll(x, step, 0), 0)
            step *= 2
        return x

    def last_row(x):
        return jnp.broadcast_to(x[x.shape[0] - 1 :, :], x.shape)

    def order(extent):
        rank = jnp.full(shape, 4096, jnp.int32)
        reach = [None] * 9
        above = asked
        for p in range(8, 0, -1):
            same = (extent == p).astype(jnp.bfloat16)
            in_group = jnp.dot(same, group, preferred_element_type=jnp.float32).astype(jnp.int32)
            ahead = jnp.dot(same, before, preferred_element_type=jnp.float32).astype(jnp.int32)
            running = running_rows(in_group)
            rank = jnp.where(extent == p, above + running - in_group + ahead, rank)
            above = above + last_row(running)
            reach[p] = above
        return rank, reach

    ways = [order(extent) for extent in (right, left)]
    wide = lambda x: jnp.concatenate((x, x), axis=0)
    reaches_wide = [[None] + [wide(x) for x in reach[1:]] for rank, reach in ways]

    def phase(t, state):
        after = []
        for way in range(2):
            rank, reach = ways[way][0], reaches_wide[way]
            going, queue, key = state[3 * way : 3 * way + 3]
            free = (going == 0).astype(jnp.int32)
            running = running_rows(free)
            nth = running - free
            number = queue + nth
            fresh = (free > 0) & (number < reach[1])
            extent = sum((number < reach[p]).astype(jnp.int32) for p in range(1, 9))
            going = jnp.where(fresh, extent, going)
            taken = jnp.minimum(queue + last_row(running), reach[1])
            mark = jnp.where(fresh, number, -1)
            for s in range(2 * SLOTS):
                here = rank == jnp.broadcast_to(mark[s : s + 1, :], shape)
                key = jnp.where(here, t * 2 * SLOTS + s, key)
            going = jnp.maximum(pltpu.roll(going, 16 if way == 0 else CODES - 16, 1) - 1, 0)
            after += [going, taken, key]
        return tuple(after)

    state = lax.fori_loop(0, PHASES, phase, (wide(zero), wide(zero), zero) * 2)
    over = wide(zero)
    for way in range(2):
        over = over + state[3 * way] + reaches_wide[way][1] - state[3 * way + 1]
    over = over[:HEADS] + over[HEADS:]
    rest[...] = over[:, :128] + over[:, 128:]

    delta = (chip - home) & (CHIPS - 1)
    core = (code >> 3) & 1
    near = ENTRIES + 2 * QUNITS + core * OWN + row * NB_DEV + (code & 7)
    goes = [(state[2] >> 4) + delta - 1, PHASES + (state[5] >> 4) + CHIPS - delta - 1]
    slots = [state[2] & 15, state[5] & 15]
    entry = [(goes[way] * 2 + (slots[way] & 1)) * SLOTS + (slots[way] >> 1) for way in range(2)]
    from_left = (delta < 8) | ((delta == 8) & (right == 8))
    far_entry = jnp.clip(jnp.where(from_left, entry[0], entry[1]), 0, ENTRIES - 1)
    where[...] = jnp.where(delta == 0, near, far_entry)

    for way in range(2):
        rank, reach = ways[way]
        sent = rank < state[3 * way + 1][:HEADS]
        keys[way] = jnp.where(sent, state[3 * way + 2], -1)
    fetch = pltpu.make_async_copy(keys, numbers, sems)
    fetch.start()
    fetch.wait()

    def clear(i, carry):
        source[i] = -1
        return carry

    lax.fori_loop(0, 2 * PHASES * SLOTS, clear, 0, unroll=8)
    base = chip * 2 * NB_DEV
    has = [chip == (first >> 4), chip == (second >> 4)]
    count = (has[0].astype(jnp.int32) + has[1].astype(jnp.int32)) * (QUNITS // G)
    for way in range(2):

        def put(i, carry):
            lane = i & 15
            key = numbers[way, i >> 4, base + lane]

            @pl.when((key >= 0) & ((key & 1) == side))
            def _():
                unit = 2 * QUNITS + (lane >> 3) * OWN + (i >> 4) * NB_DEV + (lane & 7)
                source[way * PHASES * SLOTS + (key >> 1)] = unit

            return carry

        lax.fori_loop(0, 2 * OWN, put, 0, unroll=4)
        for r in range(QUNITS):
            late = jnp.logical_not(has[0]) if r < QUNITS // G else True
            late = jnp.asarray(late)
            core = (jnp.where(late, second, first) >> 3) & 1
            unit = core * QUNITS + jnp.where(late, QUNITS // G, 0) + r % (QUNITS // G)

            @pl.when((r < count) & (side == r % 2))
            def _():
                source[way * PHASES * SLOTS + r // 2] = unit


def plan(global_ids, table, radius):
    vmem = pl.BlockSpec(memory_space=pltpu.VMEM)
    smem = pl.BlockSpec(memory_space=pltpu.SMEM)
    return pl.pallas_call(
        plan_kernel,
        in_specs=[smem, vmem, vmem],
        out_specs=(smem, vmem, vmem),
        out_shape=(
            jax.ShapeDtypeStruct((2 * PHASES * SLOTS,), jnp.int32),
            jax.ShapeDtypeStruct((HEADS, CODES), jnp.int32),
            jax.ShapeDtypeStruct((HEADS, 128), jnp.int32),
        ),
        scratch_shapes=[
            pltpu.VMEM((2, HEADS, CODES), jnp.int32),
            pltpu.SMEM((2, HEADS, CODES), jnp.int32),
            pltpu.SemaphoreType.DMA(()),
        ],
        name="plan",
    )(global_ids, table, radius)


def packet_kernel(
    source, pool, rest, log, flag, recv, stage, votes,
    send_sem, land_sem, keep_sem, across_sem, across_land, tail_sem, vote_send, vote_land,
):
    me = lax.axis_index("seq")
    chip, side = me // 2, lax.rem(me, 2)
    sibling = me + 1 - 2 * side
    ahead = lax.rem(chip + 1, CHIPS) * 2 + side
    behind = lax.rem(chip + CHIPS - 1, CHIPS) * 2 + side
    dp, tensor = lax.axis_index("dp"), lax.axis_index("tensor")
    ring = dp * 8 + tensor

    def other(k):
        there = lax.rem(ring + k, 16)
        return (there // 8, me, lax.rem(there, 8))

    greet([place(ahead), place(behind), place(sibling)] + [other(k) for k in range(1, 16)])

    def vote(k, slot):
        return pltpu.make_async_remote_copy(
            src_ref=rest,
            dst_ref=votes.at[slot],
            send_sem=vote_send.at[k],
            recv_sem=vote_land.at[k],
            device_id=other(k),
            device_id_type=MESH,
        )

    for k in range(1, 16):
        vote(k, ring).start()
    kept = pltpu.make_async_copy(pool, log.at[pl.ds(ENTRIES, UNITS)], tail_sem.at[0])
    kept.start()
    own_vote = pltpu.make_async_copy(rest, votes.at[ring], tail_sem.at[1])
    own_vote.start()

    def hop(t, way, piece):
        rows = pl.ds(piece * PIECE, PIECE)
        return pltpu.make_async_remote_copy(
            src_ref=stage.at[way, lax.rem(t, STAGES), rows],
            dst_ref=recv.at[way, t, rows],
            send_sem=send_sem.at[way, lax.rem(t, STAGES), piece],
            recv_sem=land_sem.at[way, t, piece],
            device_id=place(ahead if way == 0 else behind),
            device_id_type=MESH,
        )

    def entry(t, way, who):
        return pl.ds(((way * PHASES + t) * 2 + who) * SLOTS, SLOTS)

    def keep(t, way):
        return pltpu.make_async_copy(
            recv.at[way, t], log.at[entry(t, way, side)], keep_sem.at[way, lax.rem(t, 2)]
        )

    def across(t, way, who):
        return pltpu.make_async_remote_copy(
            src_ref=recv.at[way, t],
            dst_ref=log.at[entry(t, way, who)],
            send_sem=across_sem.at[way, lax.rem(t, 2)],
            recv_sem=across_land.at[way, t],
            device_id=place(sibling),
            device_id_type=MESH,
        )

    def compose(t, way, piece, first):
        for i in range(PIECE):
            slot = piece * PIECE + i
            wanted = source[(way * PHASES + t) * SLOTS + slot]
            unit = pool[jnp.maximum(wanted, 0)]
            if not first:
                unit = jnp.where(wanted >= 0, unit, recv[way, t - 1, slot])
            stage[way, lax.rem(t, STAGES), slot] = unit

    for piece in range(PIECES):
        for way in range(2):
            compose(0, way, piece, True)
            hop(0, way, piece).start()

    def settle(t):
        for way in range(2):
            keep(t, way).wait()
            across(t, way, side).wait_send()

    def pass_on(t):
        pl.when(t >= 2)(lambda: settle(t - 2))
        for way in range(2):
            keep(t, way).start()
            across(t, way, side).start()

    def phase(t, carry):
        def step(piece, inner):
            for way in range(2):
                hop(t - 1, way, piece).wait_recv()
                pl.when(t >= STAGES)(lambda: hop(t - STAGES, way, piece).wait_send())
                compose(t, way, piece, False)
                hop(t, way, piece).start()
            return inner

        lax.fori_loop(0, PIECES, step, 0, unroll=True)
        pass_on(t - 1)
        return carry

    lax.fori_loop(1, PHASES, phase, 0)

    def last(piece, carry):
        for way in range(2):
            hop(PHASES - 1, way, piece).wait_recv()
            for t in range(PHASES - STAGES, PHASES):
                hop(t, way, piece).wait_send()
        return carry

    lax.fori_loop(0, PIECES, last, 0)
    pass_on(PHASES - 1)
    settle(PHASES - 2)
    settle(PHASES - 1)

    def drain(t, carry):
        for way in range(2):
            across(t, way, 1 - side).wait_recv()
        return carry

    lax.fori_loop(0, PHASES, drain, 0)
    for k in range(1, 16):
        vote(k, ring).wait_send()
        vote(k, lax.rem(ring + 16 - k, 16)).wait_recv()
    kept.wait()
    own_vote.wait()
    flag[...] = jnp.max(votes[...], axis=0)


def packets(source, pool, rest):
    dma = pltpu.SemaphoreType.DMA
    vmem = pl.BlockSpec(memory_space=pltpu.VMEM)
    return pl.pallas_call(
        packet_kernel,
        in_specs=[
            pl.BlockSpec(memory_space=pltpu.SMEM),
            vmem,
            vmem,
        ],
        out_specs=(pl.BlockSpec(memory_space=pl.ANY), vmem),
        out_shape=(
            jax.ShapeDtypeStruct((ENTRIES + UNITS,) + UNIT, jnp.bfloat16),
            jax.ShapeDtypeStruct((HEADS, 128), jnp.int32),
        ),
        scratch_shapes=[
            pltpu.VMEM((2, PHASES, SLOTS) + UNIT, jnp.bfloat16),
            pltpu.VMEM((2, STAGES, SLOTS) + UNIT, jnp.bfloat16),
            pltpu.VMEM((16, HEADS, 128), jnp.int32),
            dma((2, STAGES, PIECES)),
            dma((2, PHASES, PIECES)),
            dma((2, 2)),
            dma((2, 2)),
            dma((2, PHASES)),
            dma((2,)),
            dma((16,)),
            dma((16,)),
        ],
        compiler_params=pltpu.CompilerParams(
            collective_id=1, has_side_effects=True, vmem_limit_bytes=48 * 1024 * 1024
        ),
        name="packets",
    )(source, pool, rest)


def gather_kernel(
    fast, where, wanted, info, pool, query_pool, fetched, asked, held, held_asked, sems, out_sems
):
    first = info[HEADS]

    def spot(code, h):
        if fast:
            return where[h, code]
        return (code >> 3) * OWN + h * NB_DEV + (code & 7)

    def query_spot(g, h):
        unit = g * (QUNITS // G) + h // 2
        if not fast:
            return unit
        mine = first >> 3
        owner = info[HEADS + 1 + g] >> 3
        core = owner & 1
        delta = ((mine >> 1) - (owner >> 1)) & (CHIPS - 1)
        shared = (owner >> 1) == (info[HEADS + 1] >> 4)
        rank = jnp.where(shared, unit, h // 2)
        near = ENTRIES + core * QUNITS + unit
        step = jnp.where(delta <= 8, delta - 1, PHASES + CHIPS - delta - 1)
        far = (step * 2 + (rank & 1)) * SLOTS + (rank >> 1)
        return jnp.where(delta == 0, near, far)

    def copies(h):
        for i in range(FETCH):
            if i < NEAR:
                code = jnp.clip(first - WIN + i, 0, CODES - 1)
            elif i < NEAR + G:
                code = info[HEADS + 1 + i - NEAR]
            else:
                code = wanted[h * PICKS + i - NEAR - G]
            yield pltpu.make_async_copy(pool.at[spot(code, h)], held.at[h, i], sems.at[h, i])
        for g in range(G):
            yield pltpu.make_async_copy(
                query_pool.at[query_spot(g, h), h % 2], held_asked.at[h, g], sems.at[h, FETCH + g]
            )

    def start(h, carry):
        for copy in copies(h):
            copy.start()
        return carry

    def store(h):
        return (
            pltpu.make_async_copy(held.at[h], fetched.at[h], out_sems.at[h, 0]),
            pltpu.make_async_copy(held_asked.at[h], asked.at[h], out_sems.at[h, 1]),
        )

    def pass_on(h, carry):
        for i in range(FETCH):
            pltpu.make_async_copy(pool.at[0], held.at[h, i], sems.at[h, i]).wait()
        for g in range(G):
            pltpu.make_async_copy(
                query_pool.at[0, 0], held_asked.at[h, g], sems.at[h, FETCH + g]
            ).wait()
        for copy in store(h):
            copy.start()
        return carry

    def finish(h, carry):
        for copy in store(h):
            copy.wait()
        return carry

    lax.fori_loop(0, HEADS, start, 0)
    lax.fori_loop(0, HEADS, pass_on, 0)
    lax.fori_loop(0, HEADS, finish, 0)


def gather(fast, where, wanted, info, pool, query_pool):
    smem = pl.BlockSpec(memory_space=pltpu.SMEM)
    hbm = pl.BlockSpec(memory_space=pl.ANY)
    return pl.pallas_call(
        lambda *refs: gather_kernel(fast, *refs),
        in_specs=[smem, smem, smem, hbm, hbm],
        out_specs=(hbm, hbm),
        out_shape=(
            jax.ShapeDtypeStruct((HEADS, FETCH) + UNIT, jnp.bfloat16),
            jax.ShapeDtypeStruct((HEADS, G, BLOCK, WIDTH), jnp.bfloat16),
        ),
        scratch_shapes=[
            pltpu.VMEM((HEADS, FETCH) + UNIT, jnp.bfloat16),
            pltpu.VMEM((HEADS, G, BLOCK, WIDTH), jnp.bfloat16),
            pltpu.SemaphoreType.DMA((HEADS, FETCH + G)),
            pltpu.SemaphoreType.DMA((HEADS, 2)),
        ],
        compiler_params=pltpu.CompilerParams(vmem_limit_bytes=32 * 1024 * 1024),
        name="gather" if fast else "gather_slow",
    )(where, wanted, info, pool, query_pool)


HALF = HEADS // 2
SHARE = HALF * WIDTH // CHIPS


def attend_kernel(
    info, query, pairs, asked, fetched, out, merged,
    held, part, stats, theirs, their_stats, half, half_stats, got, got_stats, piece,
    load_sem, pair_send, pair_land, send, land, send_stats, land_stats, back, home,
):
    me = lax.axis_index("seq")
    chip, side = me // 2, lax.rem(me, 2)
    sibling = me + 1 - 2 * side
    peers = [lax.rem(chip + k, CHIPS) * 2 + side for k in range(1, CHIPS)]
    first = me * NB_DEV

    def load(h):
        return pltpu.make_async_copy(fetched.at[h], held.at[h], load_sem.at[h])

    for h in range(HEADS):
        load(h).start()
    greet([place(peer) for peer in peers] + [place(sibling)])

    def pair(i, source, target):
        return pltpu.make_async_remote_copy(
            src_ref=source,
            dst_ref=target,
            send_sem=pair_send.at[i],
            recv_sem=pair_land.at[i],
            device_id=place(sibling),
            device_id_type=MESH,
        )

    column = lax.broadcasted_iota(jnp.int32, (1, LISTED * BLOCK), 1) // BLOCK - WIN
    contract = (((1,), (1,)), ((), ()))
    scale = 1.0 / math.sqrt(WIDTH)


    def one_partial(h, carry):
        own = pl.ds(h * NB_DEV, NB_DEV)
        scores = scale * lax.dot_general(
            pairs[own, 0].reshape(NB_DEV * BLOCK, WIDTH),
            asked[h].reshape(G * BLOCK, WIDTH),
            contract,
            preferred_element_type=jnp.float32,
        )
        peak = jnp.max(scores, axis=0, keepdims=True)
        weights = jnp.exp(scores - peak)
        sums = jnp.sum(weights, axis=0, keepdims=True)
        weighted = lax.dot_general(
            pairs[own, 1].reshape(NB_DEV * BLOCK, WIDTH),
            weights.astype(jnp.bfloat16),
            (((0,), (0,)), ((), ())),
            preferred_element_type=jnp.float32,
        )
        part[h] = (weighted / sums).astype(jnp.bfloat16)
        stats[h] = jnp.concatenate((peak, sums, jnp.zeros((6, WIDTH), jnp.float32)), axis=0)
        return carry

    def one_head(head, outer):
        load(head).wait()
        radius = info[head]

        def one_block(b, carry):
            rows = pl.ds(pl.multiple_of(b * BLOCK, BLOCK), BLOCK)
            units = [b + i for i in range(2 * WIN + 1)] + [NEAR, NEAR + 1]
            units = units + [NEAR + G + b * R + r for r in range(R)]
            held_keys = jnp.concatenate([held[head, i, 0] for i in units], axis=0)
            held_values = jnp.concatenate([held[head, i, 1] for i in units], axis=0)
            target = first + b + column
            inside = (jnp.abs(column) <= radius) & (target >= 0) & (target < CODES)
            usable = inside | (column > WIN)
            scores = scale * lax.dot_general(
                query[head, rows], held_keys, contract, preferred_element_type=jnp.float32
            )
            scores = jnp.where(usable, scores, -jnp.inf)
            weights = jnp.exp(scores - jnp.max(scores, axis=1, keepdims=True))
            row_total = jnp.sum(weights, axis=1, keepdims=True)
            weighted = jnp.dot(
                weights.astype(jnp.bfloat16), held_values, preferred_element_type=jnp.float32
            )
            out[head, rows] = (weighted / row_total).astype(jnp.bfloat16)
            return carry

        lax.fori_loop(0, NB_DEV, one_block, 0, unroll=4)
        return outer

    lax.fori_loop(0, HEADS, one_partial, 0, unroll=4)
    their_heads = pl.ds((1 - side) * HALF, HALF)
    my_heads = pl.ds(side * HALF, HALF)
    swaps = [
        pair(0, part.at[their_heads], theirs),
        pair(1, stats.at[their_heads], their_stats),
    ]
    for copy in swaps:
        copy.start()
    lax.fori_loop(0, 1, one_head, 0)
    for copy in swaps:
        copy.wait_recv()
    for h in range(HALF):
        mine = stats[side * HALF + h]
        other = their_stats[h]
        peak = jnp.maximum(mine[0:1, :], other[0:1, :])
        first = mine[1:2, :] * jnp.exp(mine[0:1, :] - peak)
        second = other[1:2, :] * jnp.exp(other[0:1, :] - peak)
        total = first + second
        weighted = (first / total) * part[side * HALF + h].astype(jnp.float32) + (
            second / total
        ) * theirs[h].astype(jnp.float32)
        half[h] = weighted.astype(jnp.bfloat16)
        half_stats[h : h + 1, :] = peak
        half_stats[HALF + h : HALF + h + 1, :] = total

    def rows(who):
        return who // 4, pl.ds(lax.rem(who, 4) * SHARE, SHARE)

    def hand(k, slot):
        to = lax.rem(chip + k, CHIPS)
        head, span = rows(to)
        weighted = pltpu.make_async_remote_copy(
            src_ref=half.at[head, span],
            dst_ref=got.at[slot],
            send_sem=send.at[k],
            recv_sem=land.at[k],
            device_id=place(to * 2 + side),
            device_id_type=MESH,
        )
        sums = pltpu.make_async_remote_copy(
            src_ref=half_stats,
            dst_ref=got_stats.at[slot],
            send_sem=send_stats.at[k],
            recv_sem=land_stats.at[k],
            device_id=place(to * 2 + side),
            device_id_type=MESH,
        )
        return weighted, sums

    def give(k, who):
        head, span = rows(who)
        return pltpu.make_async_remote_copy(
            src_ref=piece,
            dst_ref=merged.at[side * HALF + head, span],
            send_sem=back.at[k],
            recv_sem=home.at[k],
            device_id=place(lax.rem(chip + k, CHIPS) * 2 + side),
            device_id_type=MESH,
        )

    for k in range(1, CHIPS):
        for copy in hand(k, chip):
            copy.start()
    head, span = rows(chip)
    got[chip] = half[head, span]
    got_stats[chip] = half_stats[...]
    lax.fori_loop(1, 4, one_head, 0)
    for k in range(1, CHIPS):
        for copy in hand(k, lax.rem(chip + CHIPS - k, CHIPS)):
            copy.wait_recv()
    all_stats = got_stats[...]
    peaks = jnp.zeros((CHIPS, G * BLOCK), jnp.float32)
    sums = jnp.zeros((CHIPS, G * BLOCK), jnp.float32)
    for h in range(HALF):
        peaks = jnp.where(head == h, all_stats[:, h, :], peaks)
        sums = jnp.where(head == h, all_stats[:, HALF + h, :], sums)
    weights = sums * jnp.exp(peaks - jnp.max(peaks, axis=0, keepdims=True))
    weights = weights / jnp.sum(weights, axis=0, keepdims=True)
    total = jnp.zeros((SHARE, G * BLOCK), jnp.float32)
    for k in range(CHIPS):
        total = total + weights[k : k + 1, :] * got[k].astype(jnp.float32)
    piece[...] = total.astype(jnp.bfloat16)
    for k in range(1, CHIPS):
        give(k, chip).start()
    merged[side * HALF + head, span] = piece[...]
    lax.fori_loop(4, 7, one_head, 0)
    for k in range(1, CHIPS):
        give(k, lax.rem(chip + CHIPS - k, CHIPS)).wait_recv()
    last = pair(2, merged.at[my_heads], merged.at[my_heads])
    last.start()
    lax.fori_loop(7, HEADS, one_head, 0)
    for copy in swaps:
        copy.wait_send()
    for k in range(1, CHIPS):
        for copy in hand(k, chip):
            copy.wait_send()
        give(k, chip).wait_send()
    last.wait_send()
    pair(2, merged.at[their_heads], merged.at[their_heads]).wait_recv()


def attend(info, query, pairs, asked, fetched):
    dma = pltpu.SemaphoreType.DMA
    vmem = pl.BlockSpec(memory_space=pltpu.VMEM)
    rows = G * BLOCK
    return pl.pallas_call(
        attend_kernel,
        in_specs=[
            pl.BlockSpec(memory_space=pltpu.SMEM), vmem, vmem, vmem,
            pl.BlockSpec(memory_space=pl.ANY),
        ],
        out_specs=(vmem, vmem),
        out_shape=(
            jax.ShapeDtypeStruct((HEADS, NB_DEV * BLOCK, WIDTH), jnp.bfloat16),
            jax.ShapeDtypeStruct((HEADS, WIDTH, rows), jnp.bfloat16),
        ),
        scratch_shapes=[
            pltpu.VMEM((HEADS, FETCH) + UNIT, jnp.bfloat16),
            pltpu.VMEM((HEADS, WIDTH, rows), jnp.bfloat16),
            pltpu.VMEM((HEADS, 8, rows), jnp.float32),
            pltpu.VMEM((HALF, WIDTH, rows), jnp.bfloat16),
            pltpu.VMEM((HALF, 8, rows), jnp.float32),
            pltpu.VMEM((HALF, WIDTH, rows), jnp.bfloat16),
            pltpu.VMEM((2 * HALF, rows), jnp.float32),
            pltpu.VMEM((CHIPS, SHARE, rows), jnp.bfloat16),
            pltpu.VMEM((CHIPS, 2 * HALF, rows), jnp.float32),
            pltpu.VMEM((SHARE, rows), jnp.bfloat16),
            dma((HEADS,)),
        ]
        + [dma((3,))] * 2
        + [dma((CHIPS,))] * 6,
        compiler_params=pltpu.CompilerParams(
            collective_id=2, has_side_effects=True, vmem_limit_bytes=32 * 1024 * 1024
        ),
        name="attend",
    )(info, query, pairs, asked, fetched)


def local(queries, keys, values, window_radius, global_ids, rand_owner, rand_local):
    position = lax.axis_index("seq")
    block_ids = position * NB_DEV + jnp.arange(NB_DEV, dtype=jnp.int32)

    pairs = jnp.stack((keys, values)).reshape(2, NB_DEV, BLOCK, HEADS, WIDTH)
    pairs = pairs.transpose(3, 1, 0, 2, 4).reshape((OWN,) + UNIT)
    query_heads = queries.transpose(1, 0, 2)
    query_blocks = query_heads.reshape(HEADS, NB_DEV, BLOCK, WIDTH)
    units = jnp.concatenate(
        [
            lax.dynamic_index_in_dim(query_blocks, global_ids[g] % NB_DEV, axis=1, keepdims=False)
            for g in range(G)
        ]
    ).reshape((QUNITS,) + UNIT)
    wanted = (rand_owner[0] * NB_DEV + rand_local[0]).astype(jnp.int32)
    wanted = wanted.transpose(1, 0, 2).reshape(HEADS, PICKS)
    table, pool = exchange(jnp.pad(wanted, ((0, 0), (0, WIDTH - PICKS))), pairs, units)
    radius = jnp.broadcast_to(window_radius[:, None], (HEADS, CODES)).astype(jnp.int32)
    source, where, rest = plan(global_ids, table, radius)
    log, flag = packets(source, pool, rest)
    info = jnp.concatenate((window_radius, (position * NB_DEV)[None], global_ids)).astype(jnp.int32)
    asking = (where, wanted.reshape(-1), info)

    def from_packets(pairs, units, log):
        return gather(True, *asking, log, log)

    def from_gather(pairs, units, log):
        everything = lax.all_gather(pairs, "seq", axis=0, tiled=True)
        holder = jnp.repeat(global_ids // NB_DEV, QUNITS // G) == position
        asked = lax.psum(jnp.where(holder[:, None, None, None], units, 0), "seq")
        return gather(False, *asking, everything, asked)

    fetched, asked = lax.cond(jnp.max(flag) > 0, from_gather, from_packets, pairs, units, log)
    sparse, merged = attend(info, query_heads, pairs, asked, fetched)
    global_out = merged.reshape(HEADS, WIDTH, G, BLOCK).transpose(2, 3, 0, 1)

    result = sparse.reshape(HEADS, NB_DEV, BLOCK, WIDTH).transpose(1, 2, 0, 3)
    for slot in range(G):
        owned = global_ids[slot] == block_ids
        result = jnp.where(owned[:, None, None, None], global_out[slot][None], result)
    return result.reshape(NB_DEV * BLOCK, HEADS, WIDTH)


def solution(mesh):
    placed = (
        P(("dp", "seq"), "tensor", None),
        P(("dp", "seq"), "tensor", None),
        P(("dp", "seq"), "tensor", None),
        P(("dp", "tensor")),
        P("dp"),
        P("tensor", ("dp", "seq"), None, None),
        P("tensor", ("dp", "seq"), None, None),
    )
    return jax.shard_map(
        local,
        mesh=mesh,
        in_specs=placed,
        out_specs=P(("dp", "seq"), "tensor", None),
        check_vma=False,
    )
```
